512 devices in a mesh: pocket: 64 (over x, z, core), tensor: 8 (over y).
Axes of the slice: x: 4, y: 8, z: 8, core: 2. Of those that a mesh axis runs over, the one named last changes fastest.
Arguments:
- compound_tokens: bfloat16 [32768, 1024], P('pocket', 'tensor')
- pocket_tokens: bfloat16 [16384, 1024], P('pocket'), may hold values from -6 to 6
- token_count: int32 [512], P('pocket'), may hold values from 16 to 64
- pair_compound: int32 [64, 128], P('pocket'), may hold values from 0 to 7, never falling along the last dimension, each value on 1 to 40 neighbouring positions
- pair_conformer: int32 [8192, 1], P('pocket'), may hold values from 0 to 63; in each aligned block of 128 rows (0 to 127, 128 to 255, ...) at most 4 rows name the same one
- owner: int32 [64], replicated, may hold values from 0 to 63, each once
- w_query: bfloat16 [1024, 1024], P(None, 'tensor'), may hold values from -0.1875 to 0.1875
- w_key: bfloat16 [1024, 1024], P(None, 'tensor'), may hold values from -0.1875 to 0.1875
- w_value: bfloat16 [1024, 1024], P(None, 'tensor'), may hold values from -0.1875 to 0.1875
- w_out: bfloat16 [1024, 1024], P('tensor'), may hold values from -0.5 to 0.5
- norm_gain: float32 [1024], replicated, may hold values from 0.25 to 1.75
- w_gate: bfloat16 [1024, 4096], P(None, 'tensor'), may hold values from -0.1875 to 0.1875
- w_up: bfloat16 [1024, 4096], P(None, 'tensor'), may hold values from -0.1875 to 0.1875
- w_down: bfloat16 [4096, 1024], P('tensor'), may hold values from -0.09375 to 0.09375
Outputs:
- pair_embed: bfloat16 [8192, 1024], P('pocket', 'tensor')
The draws below stay inside these ranges and needn't reach their ends.
Inputs may be any that keep to these rules, and one draw needn't show every extreme that they name: `pair_compound`: each pocket index lists its pairs grouped by compound, in rising order; every compound has 1 to 40 pairs, one exactly 40. `pair_conformer`: among the 128 pairs of one pocket index at most 4 name the same conformer; exactly 4 do so for some conformer. Each conformer has a distinct owner.
All inputs are finite; a program needn't handle non-finite values.
Results may differ from the reference program's by a relative error of at most 0.03.
Values may be sent and summed in bfloat16 or wider, within the bound.
A program may use at most 128 MiB of HBM per device.

```python
import math
import jax
import jax.numpy as jnp
import numpy as np
from jax import lax

D = 1024
HEADS = 16
HEAD_DIM = 64
FF = 4096
TOK = 64
CONF_TOK = 256
CMP_DEV = 8
PAIR_DEV = 128
LIST_MOST = 40
CAP = 4
COMPOUNDS = 512
PAIRS = 8192
CONFORMERS = 64
N_POCKET = 64


def draw_compound_tokens(key, part):
    key = jax.random.fold_in(key, 11)
    first = jax.random.fold_in(key, 0)
    rows = COMPOUNDS * TOK
    values = jnp.clip(jax.random.normal(first, (rows, D), jnp.float32), -6.0, 6.0)
    return values.astype(jnp.bfloat16)


def with_ends(array, own_key, least, high):
    longest = array.shape.index(max(array.shape))
    spots = []
    for shift in (0, 1):
        where = [jax.random.randint(jax.random.fold_in(own_key, axis), (), 0, length) for axis, length in enumerate(array.shape)]
        where[longest] = (where[longest] + shift) % array.shape[longest]
        spots.append(tuple(where))
    return array.at[spots[0]].set(least).at[spots[1]].set(high)


def shard_levels(key, shape, cuts, smallest, largest):
    def one(axis_at, parts):
        heights = jax.random.uniform(jax.random.fold_in(jax.random.fold_in(key, 6), axis_at), (parts,), jnp.float32, smallest / len(cuts), largest / len(cuts))
        return jnp.repeat(jnp.exp(heights), shape[axis_at] // parts).reshape((-1,) + (1,) * (len(shape) - axis_at - 1))

    level = one(*cuts[0])
    for cut in cuts[1:]:
        level = level * one(*cut)
    return level


def profile(amount, total, reach, slope):
    loads = [(1 << 20) // math.isqrt(grade ** slope) + 1 for grade in range(2, amount + 1)]
    spare, given = total - reach - (amount - 1), [1] * (amount - 1)
    while spare > 0:
        candidates = [i for i in range(amount - 1) if given[i] < reach]
        pool, budget = sum([loads[i] for i in candidates]), spare
        for i in candidates:
            more = min(reach - given[i], max(1, budget * loads[i] // pool), spare)
            given[i] = given[i] + more
            spare = spare - more
    return np.array([reach] + given)


def uneven_parts(rng, amount, total, limit, skew):
    if amount == 2:
        one = jax.random.randint(rng, (), max(1, total - limit), min(limit, total - 1) + 1)
        return jnp.stack([one, total - one])
    lengths = jnp.asarray(profile(amount, total, limit, skew), jnp.int32)
    twos = (amount - 1) // 2
    source_of, receiver = lengths[1:1 + 2 * twos:2], lengths[2:2 + 2 * twos:2]
    room = jnp.minimum(source_of - 1, limit - receiver)
    moved = jax.random.randint(jax.random.fold_in(rng, 1), (twos,), 0, 1 << 20) % (room + 1)
    lengths = lengths.at[1:1 + 2 * twos:2].set(source_of - moved).at[2:2 + 2 * twos:2].set(receiver + moved)
    return lengths[jax.random.permutation(jax.random.fold_in(rng, 2), amount)]


def routed_block(key, own, number, rows, number_of, top, limit, skew):
    sequence = jax.random.permutation(key, number_of)
    crowded, ordinary = shares(number_of, rows * top, limit, skew, True), shares(number_of, rows * top, limit, skew, False)
    places = jnp.arange(number_of)

    def named(tallies, rotation):
        used = int((tallies > 0).sum())
        fixed = max(1, used // 4)
        moved = fixed + (places - fixed + rotation * (used - fixed)) % max(1, number_of - fixed)
        return jnp.zeros((number_of,), jnp.int32).at[sequence[jnp.where(places < fixed, places, moved)]].set(jnp.asarray(tallies, jnp.int32))

    tallies = jnp.where(number % 4 == 0, named(crowded, number // 4), named(ordinary, number - number // 4 - 1))
    mixed = jax.random.permutation(jax.random.fold_in(own, 3), number_of)
    giver, taker = mixed[0:number_of // 2 * 2:2], mixed[1:number_of // 2 * 2:2]
    room = jnp.minimum(tallies[giver] - 1, limit - tallies[taker]) // 2
    room = jnp.where((giver == sequence[0]) | (taker == sequence[0]) | (tallies[taker] == 0), 0, jnp.maximum(room, 0))
    moved = jax.random.randint(jax.random.fold_in(own, 4), (number_of // 2,), 0, 1 << 20) % (room + 1)
    tallies = tallies.at[giver].add(-moved).at[taker].add(moved)
    items = jnp.searchsorted(jnp.cumsum(tallies), jnp.arange(rows * top), side="right").astype(jnp.int32)
    table = items.reshape(top, rows).T
    table = table[jax.random.permutation(jax.random.fold_in(own, 1), rows)]
    rotation = jax.random.randint(jax.random.fold_in(own, 2), (rows, 1), 0, top)
    return jnp.take_along_axis(table, (jnp.arange(top)[None, :] + rotation) % top, axis=1)


def shares(count, total, limit, lean, full):
    loads = [(1 << 20) // math.isqrt(standing ** lean) + 1 for standing in range(1, count + 1)]
    largest = limit if full else min(limit, max(-(-total // count), total * loads[0] // sum(loads)))
    least = 1 if total - largest >= count - 1 else 0
    holding, surplus = [largest] + [least] * (count - 1), total - largest - least * (count - 1)
    while surplus > 0:
        movable = [i for i in range(1, count) if holding[i] < largest] or [i for i in range(1, count) if holding[i] < limit]
        mass, left = sum([loads[i] for i in movable]), surplus
        for i in movable:
            extra = min(limit - holding[i], max(1, left * loads[i] // mass), surplus)
            holding[i] = holding[i] + extra
            surplus = surplus - extra
    return np.array(holding)


def gaussian(rng, extent, deviation, bound, shards=(), kind=jnp.bfloat16):
    entries = deviation * jax.random.normal(rng, extent, jnp.float32)
    if shards:
        entries = entries * shard_levels(rng, extent, shards, -0.22, 0.18)
    return jnp.clip(entries, -bound, bound).astype(kind)


def setup_inputs(seed: int = 0) -> dict:
    key_of = jax.random.split(jax.random.key(seed), 15)
    compound_tokens = draw_compound_tokens(jax.random.fold_in(key_of[14], 71), 0)
    pocket_tokens = gaussian(key_of[1], (CONFORMERS * CONF_TOK, D), 1.0, 6.0, ((0, 64),))
    token_count = with_ends(jax.random.randint(key_of[2], (COMPOUNDS,), TOK // 4, TOK + 1), jax.random.fold_in(key_of[2], 1), TOK // 4, TOK).astype(jnp.int32)
    pair_compound = jax.vmap(lambda own: jnp.searchsorted(jnp.cumsum(uneven_parts(own, CMP_DEV, PAIR_DEV, LIST_MOST, 2)), jnp.arange(PAIR_DEV), side="right"))(jax.random.split(key_of[3], N_POCKET)).reshape((N_POCKET, PAIR_DEV)).astype(jnp.int32)
    pair_conformer_keys = jax.random.split(jax.random.fold_in(key_of[4], 1), PAIRS // PAIR_DEV)
    pair_conformer_turns = jax.random.permutation(jax.random.fold_in(key_of[4], 3), PAIRS // PAIR_DEV)
    pair_conformer = jax.vmap(lambda own, number: routed_block(jax.random.fold_in(key_of[4], 2), own, number, PAIR_DEV, CONFORMERS, 1, CAP, 2))(pair_conformer_keys, pair_conformer_turns).reshape((PAIRS, 1))
    owner = jax.random.permutation(key_of[5], CONFORMERS).astype(jnp.int32)
    w_query = gaussian(key_of[6], (D, HEADS * HEAD_DIM), D ** -0.5, 0.1875, ((1, 8),))
    w_key = gaussian(key_of[7], (D, HEADS * HEAD_DIM), D ** -0.5, 0.1875, ((1, 8),))
    w_value = gaussian(key_of[8], (D, HEADS * HEAD_DIM), D ** -0.5, 0.1875, ((1, 8),))
    w_out = gaussian(key_of[9], (HEADS * HEAD_DIM, D), (HEADS * HEAD_DIM // 8) ** -0.5, 0.5, ((0, 8),))
    norm_gain = jnp.clip(1.0 + 0.15 * jax.random.normal(key_of[10], (D,), jnp.float32), 0.25, 1.75)
    w_gate = gaussian(key_of[11], (D, FF), D ** -0.5, 0.1875, ((1, 8),))
    w_up = gaussian(key_of[12], (D, FF), D ** -0.5, 0.1875, ((1, 8),))
    w_down = gaussian(key_of[13], (FF, D), FF ** -0.5, 0.09375, ((0, 8),))
    return {"compound_tokens": compound_tokens, "pocket_tokens": pocket_tokens, "token_count": token_count, "pair_compound": pair_compound, "pair_conformer": pair_conformer, "owner": owner, "w_query": w_query, "w_key": w_key, "w_value": w_value, "w_out": w_out, "norm_gain": norm_gain, "w_gate": w_gate, "w_up": w_up, "w_down": w_down}


def reference(compound_tokens, pocket_tokens, token_count, pair_compound, pair_conformer, owner, w_query, w_key, w_value, w_out, norm_gain, w_gate, w_up, w_down):
    queries = jnp.dot(compound_tokens, w_query, preferred_element_type=jnp.float32).astype(jnp.bfloat16)
    queries = queries.reshape(COMPOUNDS, TOK, HEADS, HEAD_DIM)
    key_rows = jnp.dot(pocket_tokens, w_key, preferred_element_type=jnp.float32).astype(jnp.bfloat16)
    key_rows = key_rows.reshape(CONFORMERS, CONF_TOK, HEADS, HEAD_DIM)
    value_rows = jnp.dot(pocket_tokens, w_value, preferred_element_type=jnp.float32).astype(jnp.bfloat16)
    value_rows = value_rows.reshape(CONFORMERS, CONF_TOK, HEADS, HEAD_DIM)
    offsets = (jnp.arange(N_POCKET, dtype=jnp.int32) * CMP_DEV)[:, None]
    compound_ids = (pair_compound + offsets).reshape(PAIRS).astype(jnp.int32)
    owner_rows = owner[pair_conformer[:, 0]].astype(jnp.int32)
    valid_mask = (jnp.arange(TOK, dtype=jnp.int32)[None, :] < token_count[:, None]).astype(jnp.float32)
    counts = token_count.astype(jnp.float32)
    score_scale = HEAD_DIM ** (-0.5)

    def one_batch(ids):
        comp_batch, owner_batch = ids
        q_part = queries[comp_batch].astype(jnp.float32)
        k_part = key_rows[owner_batch].astype(jnp.float32)
        v_part = value_rows[owner_batch].astype(jnp.float32)
        scores = jnp.einsum('btha,bsha->bhts', q_part, k_part) * score_scale
        probs = jax.nn.softmax(scores, axis=-1).astype(jnp.bfloat16)
        attended = jnp.einsum('bhts,bsha->btha', probs.astype(jnp.float32), v_part).astype(jnp.bfloat16)
        pooled = jnp.einsum('bt,btha->bha', valid_mask[comp_batch], attended.astype(jnp.float32))
        pooled = pooled / counts[comp_batch][:, None, None]
        return pooled.reshape(comp_batch.shape[0], HEADS * HEAD_DIM)
    pooled_attn = lax.map(one_batch, (compound_ids.reshape(N_POCKET, PAIR_DEV), owner_rows.reshape(N_POCKET, PAIR_DEV)))
    pooled_attn = pooled_attn.reshape(PAIRS, HEADS * HEAD_DIM).astype(jnp.bfloat16)
    x_pooled = jnp.einsum('ct,ctd->cd', valid_mask, compound_tokens.astype(jnp.float32).reshape(COMPOUNDS, TOK, D))
    x_pooled = x_pooled / counts[:, None]
    mixed = x_pooled[compound_ids] + jnp.dot(pooled_attn, w_out, preferred_element_type=jnp.float32)
    normed = mixed * lax.rsqrt(lax.optimization_barrier(jnp.mean(mixed * mixed, axis=-1, keepdims=True)) + 1e-05) * norm_gain
    normed = normed.astype(jnp.bfloat16)
    gate_proj = jnp.dot(normed, w_gate, preferred_element_type=jnp.float32)
    up_proj = jnp.dot(normed, w_up, preferred_element_type=jnp.float32)
    hidden = (jax.nn.silu(gate_proj) * up_proj).astype(jnp.bfloat16)
    return (mixed + jnp.dot(hidden, w_down, preferred_element_type=jnp.float32)).astype(jnp.bfloat16)
```

```python
import functools

import jax
import jax.numpy as jnp
from jax import lax
from jax.experimental import pallas as pl
from jax.experimental.pallas import tpu as pltpu
from jax.sharding import PartitionSpec as P

HEAD_DIM = 64
BATCH = 8


def attend_kernel(comp_ref, block_ref, qt_ref, weight_ref, k_ref, v_ref, out_ref):
    lane = lax.broadcasted_iota(jnp.int32, (8, 128), 1)
    row = lax.broadcasted_iota(jnp.int32, (8, 128), 0)
    own_head = (lane // HEAD_DIM) == row
    low_lane = lax.broadcasted_iota(jnp.int32, (1, 128), 1) < HEAD_DIM

    def step(i, carry):
        rows = []
        for j in range(BATCH):
            c = comp_ref[i * BATCH + j]
            b = block_ref[i * BATCH + j]
            scores = jnp.dot(k_ref[b], qt_ref[c], preferred_element_type=jnp.float32)
            probs = jnp.exp(scores - jnp.max(scores, axis=0, keepdims=True))
            share = weight_ref[c] / jnp.sum(probs, axis=0, keepdims=True)
            share = jnp.where(own_head, share, 0.0).astype(jnp.bfloat16)
            pooled_probs = lax.dot_general(
                share,
                probs.astype(jnp.bfloat16),
                (((1,), (1,)), ((), ())),
                preferred_element_type=jnp.float32,
            )
            values = jnp.dot(
                pooled_probs.astype(jnp.bfloat16), v_ref[b], preferred_element_type=jnp.float32
            )
            rows.append(jnp.where(low_lane, values[0:1], values[1:2]))
        out_ref[pl.ds(pl.multiple_of(i * BATCH, BATCH), BATCH), :] = jnp.concatenate(rows, axis=0)
        return carry

    lax.fori_loop(0, out_ref.shape[0] // BATCH, step, 0)


def local(
    compound_tokens,
    pocket_tokens,
    token_count,
    pair_compound,
    pair_conformer,
    owner,
    w_query,
    w_key,
    w_value,
    w_out,
    norm_gain,
    w_gate,
    w_up,
    w_down,
):
    f32, bf16 = jnp.float32, jnp.bfloat16
    cmp_dev = token_count.shape[0]
    keys = jnp.dot(pocket_tokens, w_key, preferred_element_type=f32).astype(bf16)
    all_keys = lax.all_gather(keys, "pocket", axis=0)
    values = jnp.dot(pocket_tokens, w_value, preferred_element_type=f32).astype(bf16)
    all_values = lax.all_gather(values, "pocket", axis=0)
    gathered = lax.all_gather(compound_tokens, "tensor", axis=1, tiled=True)
    tok_rows = gathered.shape[0] // cmp_dev
    queries = jnp.dot(gathered, w_query, preferred_element_type=f32).astype(bf16)
    queries = queries.reshape(cmp_dev, tok_rows, 2, HEAD_DIM) * (HEAD_DIM**-0.5)
    eye = jnp.eye(2, dtype=f32)
    qt = jnp.einsum("cthd,hg->chdgt", queries.astype(f32), eye).astype(bf16)
    qt = qt.reshape(cmp_dev, 128, 128)
    comp = pair_compound[0]
    block = owner[pair_conformer[:, 0]]
    counts = token_count.astype(f32)
    valid = (jnp.arange(tok_rows, dtype=jnp.int32)[None, :] < token_count[:, None]).astype(f32)
    weight = valid / counts[:, None]
    weight2 = jnp.concatenate([weight, weight], axis=1)[:, None, :]
    pooled_attn = pl.pallas_call(
        attend_kernel,
        out_shape=jax.ShapeDtypeStruct((comp.shape[0], 128), f32),
        in_specs=[pl.BlockSpec(memory_space=pltpu.SMEM)] * 2
        + [pl.BlockSpec(memory_space=pltpu.VMEM)] * 4,
        out_specs=pl.BlockSpec(memory_space=pltpu.VMEM),
        compiler_params=pltpu.CompilerParams(vmem_limit_bytes=48 << 20),
        name="pooled_attention",
    )(comp, block, qt, weight2, all_keys, all_values)
    x_compound = jnp.einsum(
        "ct,ctd->cd",
        valid.astype(bf16),
        gathered.reshape(cmp_dev, tok_rows, -1),
        preferred_element_type=f32,
    ) / counts[:, None]
    comp_hot = (comp[:, None] == jnp.arange(cmp_dev, dtype=jnp.int32)[None, :]).astype(f32)
    x_pair = jnp.dot(comp_hot, x_compound, precision=lax.Precision.HIGHEST)
    head_terms = jnp.dot(pooled_attn.astype(bf16), w_out, preferred_element_type=f32)
    mixed = x_pair + lax.psum(head_terms.astype(bf16), "tensor").astype(f32)
    normed = mixed * lax.rsqrt(jnp.mean(mixed * mixed, axis=-1, keepdims=True) + 1e-05) * norm_gain
    normed = normed.astype(bf16)
    gate_proj = jnp.dot(normed, w_gate, preferred_element_type=f32)
    up_proj = jnp.dot(normed, w_up, preferred_element_type=f32)
    hidden = (jax.nn.silu(gate_proj) * up_proj).astype(bf16)
    down_terms = jnp.dot(hidden, w_down, preferred_element_type=f32)
    ffn_share = lax.psum_scatter(
        down_terms.astype(bf16), "tensor", scatter_dimension=1, tiled=True
    ).astype(f32)
    out_width = ffn_share.shape[1]
    mixed_share = lax.dynamic_slice_in_dim(
        mixed, lax.axis_index("tensor") * out_width, out_width, 1
    )
    return (mixed_share + ffn_share).astype(bf16)


def solution(mesh):
    return jax.shard_map(
        local,
        mesh=mesh,
        in_specs=(
            P("pocket", "tensor"),
            P("pocket", None),
            P("pocket"),
            P("pocket", None),
            P("pocket", None),
            P(),
            P(None, "tensor"),
            P(None, "tensor"),
            P(None, "tensor"),
            P("tensor", None),
            P(),
            P(None, "tensor"),
            P(None, "tensor"),
            P("tensor", None),
        ),
        out_specs=P("pocket", "tensor"),
        check_vma=False,
    )
```

```python
import jax
import jax.numpy as jnp
from jax import lax
from jax.experimental import pallas as pl
from jax.experimental.pallas import tpu as pltpu
from jax.sharding import PartitionSpec as P

MESH = pl.DeviceIdType.MESH
NX, NZ, NT = 4, 8, 8
HEAD_DIM = 64
CMP, TOK, KEYS, WIDTH, PAIRS = 8, 64, 256, 128, 128
D, FFN = 1024, 512
SPLIT = 112
BATCH = 16
LOG2E = 1.4426950408889634
F32, BF16 = jnp.float32, jnp.bfloat16
NT_DIMS = (((1,), (1,)), ((), ()))


def guard(cond, fn):
    if isinstance(cond, bool):
        if cond:
            fn()
    else:
        pl.when(cond)(fn)


def both(*conds):
    out = True
    for cond in conds:
        if isinstance(cond, bool):
            if not cond:
                return False
        else:
            out = cond if out is True else jnp.logical_and(out, cond)
    return out


class Place:
    def __init__(self):
        p = lax.axis_index("pocket")
        self.y = lax.axis_index("tensor")
        self.c = lax.rem(p, 2)
        chip = lax.div(p, 2)
        self.z = lax.rem(chip, NZ)
        self.x = lax.div(chip, NZ)
        self.d = 1 - 2 * self.c
        self.next_x = self.pocket(self.at_x(-1), self.z)
        self.prev_x = self.pocket(self.at_x(1), self.z)
        self.next_z = self.pocket(self.x, self.at_z(-1))
        self.prev_z = self.pocket(self.x, self.at_z(1))
        self.sibling = p + self.d

    def pocket(self, x, z):
        return (x * NZ + z) * 2 + self.c

    def at_x(self, i):
        return lax.rem(self.x - i * self.d + 2 * NX, NX)

    def at_z(self, j):
        return lax.rem(self.z - j * self.d + 2 * NZ, NZ)

    def at_y(self, s):
        return lax.rem(self.y + s + 2 * NT, NT)


class Gather:
    def __init__(self, at, buf, sems):
        self.at, self.buf = at, buf
        self.ax, self.az, self.bz, self.bx, self.sa, self.sb = sems

    def low(self, j, i):
        return self.buf.at[self.at.c, self.at.at_z(j), self.at.at_x(i), 0:SPLIT]

    def high(self, j, i):
        return self.buf.at[self.at.c, self.at.at_z(j), self.at.at_x(i), SPLIT:KEYS]

    def copy(self, ref, sem, pocket):
        return pltpu.make_async_remote_copy(
            src_ref=ref,
            dst_ref=ref,
            send_sem=sem[0],
            recv_sem=sem[1],
            device_id=(pocket, self.at.y),
            device_id_type=MESH,
        )

    def sem(self, pair, *index):
        return pair.at[(0,) + index], pair.at[(1,) + index]

    def low_x(self, i, arrived=False):
        return self.copy(self.low(0, i if arrived else i - 1), self.sem(self.ax, i - 1), self.at.next_x)

    def low_z(self, k, r, arrived=False):
        return self.copy(self.low(r if arrived else r - 1, k), self.sem(self.az, k, r - 1), self.at.next_z)

    def high_z(self, r, arrived=False):
        return self.copy(self.high(r if arrived else r - 1, 0), self.sem(self.bz, r - 1), self.at.next_z)

    def high_x(self, j, i, arrived=False):
        return self.copy(self.high(j, i if arrived else i - 1), self.sem(self.bx, j, i - 1), self.at.next_x)

    def over_low(self, j, arrived=False):
        c = 1 - self.at.c if arrived else self.at.c
        z = lax.rem(self.at.z + j * self.at.d + 2 * NZ, NZ) if arrived else self.at.at_z(j)
        return self.copy(self.buf.at[c, z, :, 0:SPLIT], self.sem(self.sa, j), self.at.sibling)

    def over_high(self, j, arrived=False):
        c = 1 - self.at.c if arrived else self.at.c
        z = lax.rem(self.at.z + j * self.at.d + 2 * NZ, NZ) if arrived else self.at.at_z(j)
        return self.copy(self.buf.at[c, z, :, SPLIT:KEYS], self.sem(self.sb, j), self.at.sibling)

    def round(self, t):
        def along_x():
            guard(t > 1, lambda: self.low_x(t - 1, True).wait_recv())
            guard(t < NX, lambda: self.low_x(t).start())

        guard(t <= NX, along_x)
        for k in range(NX):
            def chain(k=k):
                guard(t > k + 1, lambda: self.low_z(k, t - k - 1, True).wait_recv())
                guard(t < k + NZ, lambda: self.low_z(k, t - k).start())

            guard(both(t > k, t <= k + NZ), chain)
        guard(t >= NX, lambda: self.over_low(t - NX).start())

        def along_z():
            guard(t > 1, lambda: self.high_z(t - 1, True).wait_recv())
            guard(t < NZ, lambda: self.high_z(t).start())

        guard(t <= NZ, along_z)
        for i in range(1, NX + 1):
            def hop(i=i):
                if i > 1:
                    self.high_x(t - i, i - 1, True).wait_recv()
                if i < NX:
                    self.high_x(t - i, i).start()
                else:
                    self.over_high(t - i).start()

            guard(both(t >= i, t < i + NZ), hop)

    def sends(self):
        out = [self.low_x(i) for i in range(1, NX)]
        out += [self.low_z(k, r) for k in range(NX) for r in range(1, NZ)]
        out += [self.high_z(r) for r in range(1, NZ)]
        out += [self.high_x(j, i) for j in range(NZ) for i in range(1, NX)]
        out += [self.over_low(j) for j in range(NZ)] + [self.over_high(j) for j in range(NZ)]
        return out

    def finish(self):
        for j in range(NZ):
            self.over_low(j, True).wait_recv()
            self.over_high(j, True).wait_recv()


class Ring:
    LAST = ((4, 3), (3, 4))

    def __init__(self, at, piece, sems):
        self.at, self.piece, self.sems = at, piece, sems

    def copy(self, half, way, s, arrived=False):
        hop = s if arrived else s - 1
        ref = self.piece(self.at.at_y(-hop if way == 0 else hop), half)
        return pltpu.make_async_remote_copy(
            src_ref=ref,
            dst_ref=ref,
            send_sem=self.sems.at[0, half, way, s - 1],
            recv_sem=self.sems.at[1, half, way, s - 1],
            device_id=(lax.axis_index("pocket"), self.at.at_y(1 if way == 0 else -1)),
            device_id_type=MESH,
        )

    def step(self, s):
        for half in range(2):
            for way in range(2):
                if 1 < s <= self.LAST[half][way] + 1:
                    self.copy(half, way, s - 1, True).wait_recv()
                if s <= self.LAST[half][way]:
                    self.copy(half, way, s).start()

    def sends(self):
        return [
            self.copy(half, way, s)
            for half in range(2)
            for way in range(2)
            for s in range(1, self.LAST[half][way] + 1)
        ]


def kernel(
    count_s, comp_s, conf_s, owner_s, comp_v, gain_v,
    x_hbm, pt_hbm, wq_hbm, wk_hbm, wv_hbm, wo_hbm, wg_hbm, wu_hbm, wd_hbm,
    out_ref,
    kbuf, vbuf, xbuf, wbuf, pt, wq, wk, wv, wg, wu, wd,
    qt, wt, xm, score, expo, pp, pg, mixed_ref, ds, rs,
    load_sem, k_ax, k_az, k_bz, k_bx, k_sa, k_sb, v_ax, v_az, v_bz, v_bx, v_sa, v_sb,
    x_sem, w_sem, ws_sem, g_sem, r_sem,
):
    at = Place()
    y = at.y
    p = lax.axis_index("pocket")

    def load(i, src, dst):
        copy = pltpu.make_async_copy(src, dst, load_sem.at[i])
        copy.start()
        return copy

    l_pt = load(0, pt_hbm, pt)
    l_wk = load(1, wk_hbm, wk)
    l_x = load(2, x_hbm, xbuf.at[y])
    l_wv = load(3, wv_hbm, wv)
    l_wq = load(4, wq_hbm, wq)
    l_wo = load(5, wo_hbm, wbuf.at[y])
    l_wg = load(6, wg_hbm, wg)
    l_wu = load(7, wu_hbm, wu)
    l_wd = load(8, wd_hbm, wd)

    barrier = pltpu.get_barrier_semaphore()
    for pocket in (at.next_x, at.prev_x, at.next_z, at.prev_z, at.sibling):
        pl.semaphore_signal(barrier, inc=1, device_id=(pocket, y), device_id_type=MESH)
    for s in range(1, NT):
        pl.semaphore_signal(barrier, inc=1, device_id=(p, at.at_y(s)), device_id_type=MESH)

    gk = Gather(at, kbuf, (k_ax, k_az, k_bz, k_bx, k_sa, k_sb))
    gv = Gather(at, vbuf, (v_ax, v_az, v_bz, v_bx, v_sa, v_sb))
    rx = Ring(at, lambda t, half: xbuf.at[t, pl.ds(half * 256, 256)], x_sem)
    rw = Ring(at, lambda t, half: wbuf.at[t, pl.ds(at.c * 64 + half * 32, 32)], w_sem)

    def hand_w(t, i):
        ref = wbuf.at[t, pl.ds(at.c * 64, 64)]
        return pltpu.make_async_remote_copy(
            src_ref=ref, dst_ref=ref, send_sem=ws_sem.at[0, i], recv_sem=ws_sem.at[1, i],
            device_id=(at.sibling, y), device_id_type=MESH,
        )

    def hand_w_arrived(t, i):
        ref = wbuf.at[t, pl.ds((1 - at.c) * 64, 64)]
        return pltpu.make_async_remote_copy(
            src_ref=ref, dst_ref=ref, send_sem=ws_sem.at[0, i], recv_sem=ws_sem.at[1, i],
            device_id=(at.sibling, y), device_id_type=MESH,
        )

    l_pt.wait()
    l_wk.wait()
    kbuf[at.c, at.z, at.x] = jnp.dot(pt[...], wk[...], preferred_element_type=F32).astype(BF16)
    pl.semaphore_wait(barrier, 5 + NT - 1)
    gk.round(1)
    l_x.wait()
    rx.step(1)
    l_wv.wait()
    vbuf[at.c, at.z, at.x] = jnp.dot(pt[...], wv[...], preferred_element_type=F32).astype(BF16)
    for t in range(2, 8):
        gk.round(t)
        if t in (3, 5, 7):
            rx.step((t + 1) // 2)
    for t in range(8, 11):
        gk.round(t)
        gv.round(t - 7)

    rx.step(5)
    l_wo.wait()
    rw.step(1)
    l_wq.wait()
    lane = lax.broadcasted_iota(jnp.int32, (1, WIDTH), 1)
    lane_tok = lax.rem(lane, HEAD_DIM)
    row_x = lax.broadcasted_iota(jnp.int32, (16, CMP * TOK), 0)
    lane_x = lax.broadcasted_iota(jnp.int32, (16, CMP * TOK), 1)
    row8 = lax.broadcasted_iota(jnp.int32, (16, 1), 0)
    valid = jnp.zeros((16, CMP * TOK), jnp.bool_)
    count_col = jnp.ones((16, 1), F32)
    for c in range(CMP):
        n = count_s[c]
        nf = n.astype(F32)
        wt[c] = jnp.where(lane_tok < n, 1.0 / jnp.full((1, WIDTH), nf), 0.0)
        valid = jnp.logical_or(
            valid,
            jnp.logical_and(row_x == c, jnp.logical_and(lane_x >= c * TOK, lane_x < c * TOK + n)),
        )
        count_col = jnp.where(row8 == c, nf, count_col)
    valid = jnp.where(valid, 1.0, 0.0).astype(BF16)
    q = jnp.zeros((CMP * TOK, WIDTH), F32)
    for t in range(NT):
        q = q + jnp.dot(xbuf[t], wq[pl.ds(t * WIDTH, WIDTH), :], preferred_element_type=F32)
        xm[:, t * WIDTH : (t + 1) * WIDTH] = (
            jnp.dot(valid, xbuf[t], preferred_element_type=F32) / count_col
        )
    q = q * (HEAD_DIM**-0.5 * LOG2E)
    low_lane = lane < HEAD_DIM
    for c in range(CMP):
        one = q[c * TOK : (c + 1) * TOK]
        block = jnp.concatenate(
            [jnp.where(low_lane, one, 0.0), jnp.where(low_lane, 0.0, one)], axis=0
        )
        qt[c] = block.T.astype(BF16)
    gk.round(11)
    gk.finish()

    own_head = (
        lax.broadcasted_iota(jnp.int32, (16, WIDTH), 1) // HEAD_DIM
        == lax.broadcasted_iota(jnp.int32, (16, WIDTH), 0)
    )

    def block_of(i):
        b = owner_s[conf_s[i]]
        return lax.bitwise_and(b, 1), lax.bitwise_and(lax.shift_right_logical(b, 1), 7), lax.shift_right_logical(b, 4)

    def attend(u, carry):
        gv.round(u)
        for s, when in ((2, 5), (3, 7), (4, 9), (5, 11)):
            def forward(s=s):
                rw.step(s)
                if s < 5:
                    hand_w(at.at_y(-(s - 1)), 2 * (s - 2)).start()
                    hand_w(at.at_y(s - 1), 2 * (s - 2) + 1).start()
                else:
                    hand_w(at.at_y(4), 6).start()

            pl.when(u == when)(forward)
        i = u - 4
        peaks, sums = [], []
        for j in range(BATCH):
            c, z, x = block_of(i * BATCH + j)
            s = jnp.dot(kbuf[c, z, x], qt[comp_s[0, i * BATCH + j]], preferred_element_type=F32)
            score[j] = s
            peaks.append(jnp.max(s, axis=0, keepdims=True))
        for j in range(BATCH):
            e = jnp.exp2(score[j] - peaks[j])
            sums.append(jnp.sum(e, axis=0, keepdims=True))
            expo[j] = e.astype(BF16)
        for j in range(BATCH):
            share = wt[comp_s[0, i * BATCH + j]] / sums[j]
            share = jnp.where(own_head, share, 0.0).astype(BF16)
            pp[i * BATCH + j] = lax.dot_general(
                share, expo[j], NT_DIMS, preferred_element_type=F32
            ).astype(BF16)
        return carry

    lax.fori_loop(4, 12, attend, 0)
    gv.finish()

    def weigh(i, carry):
        rows = []
        for j in range(BATCH):
            c, z, x = block_of(i * BATCH + j)
            v = jnp.dot(pp[i * BATCH + j], vbuf[c, z, x], preferred_element_type=F32)
            rows.append(jnp.where(low_lane, v[0:1], v[1:2]))
        pg[y, pl.ds(pl.multiple_of(i * BATCH, BATCH), BATCH), :] = jnp.concatenate(
            rows, axis=0
        ).astype(BF16)
        return carry

    lax.fori_loop(0, PAIRS // BATCH, weigh, 0)

    def to_peer(src, dst, sems, s):
        return pltpu.make_async_remote_copy(
            src_ref=src, dst_ref=dst, send_sem=sems.at[0, s - 1], recv_sem=sems.at[1, s - 1],
            device_id=(p, at.at_y(s)), device_id_type=MESH,
        )

    order = (4, 3, 5, 2, 6, 1, 7)
    for s in order:
        to_peer(pg.at[y], pg.at[y], g_sem, s).start()
    for copy in gk.sends() + gv.sends() + rx.sends() + rw.sends():
        copy.wait_send()
    for s in range(1, 5):
        for i, t in ((2 * s - 2, -s), (2 * s - 1, s)):
            if i < 7:
                hand_w(at.at_y(t), i).wait_send()
                hand_w_arrived(at.at_y(t), i).wait_recv()
    hot = (lax.broadcasted_iota(jnp.int32, (WIDTH, PAIRS), 0) == comp_v[...]).astype(F32).T
    table = jnp.concatenate([xm[0:CMP], jnp.zeros((WIDTH - CMP, D), F32)], axis=0)
    x_pair = jnp.dot(hot, table, precision=lax.Precision.HIGHEST, preferred_element_type=F32)
    l_wg.wait()
    l_wu.wait()
    l_wd.wait()
    for s in range(1, NT):
        to_peer(pg.at[y], pg.at[at.at_y(-s)], g_sem, s).wait_recv()
    mixed = x_pair
    for t in range(NT):
        mixed = mixed + jnp.dot(pg[t], wbuf[t], preferred_element_type=F32)
    for t in range(NT):
        mixed_ref[t] = mixed[:, t * WIDTH : (t + 1) * WIDTH]
    scale = lax.rsqrt(jnp.mean(mixed * mixed, axis=1, keepdims=True) + 1e-05)
    normed = (mixed * scale * gain_v[...]).astype(BF16)
    gate = jnp.dot(normed, wg[...], preferred_element_type=F32)
    up = jnp.dot(normed, wu[...], preferred_element_type=F32)
    hidden = (gate / (1.0 + jnp.exp(-gate)) * up).astype(BF16)
    for t in range(NT):
        ds[t] = jnp.dot(
            hidden, wd[:, t * WIDTH : (t + 1) * WIDTH], preferred_element_type=F32
        ).astype(BF16)
    for s in order:
        to_peer(ds.at[at.at_y(s)], rs.at[y], r_sem, s).start()
    total = ds[y].astype(F32)
    for s in order:
        to_peer(pg.at[y], pg.at[y], g_sem, s).wait_send()
    for s in order:
        from_y = at.at_y(-s)
        to_peer(ds.at[y], rs.at[from_y], r_sem, s).wait_recv()
        total = total + rs[from_y].astype(F32)
    out_ref[...] = (mixed_ref[y] + total).astype(BF16)
    for s in order:
        to_peer(ds.at[at.at_y(s)], rs.at[y], r_sem, s).wait_send()


def local(
    compound_tokens,
    pocket_tokens,
    token_count,
    pair_compound,
    pair_conformer,
    owner,
    w_query,
    w_key,
    w_value,
    w_out,
    norm_gain,
    w_gate,
    w_up,
    w_down,
):
    smem = pl.BlockSpec(memory_space=pltpu.SMEM)
    vmem = pl.BlockSpec(memory_space=pltpu.VMEM)
    hbm = pl.BlockSpec(memory_space=pl.ANY)
    dma = pltpu.SemaphoreType.DMA
    gather_sems = [
        dma((2, NX - 1)), dma((2, NX, NZ - 1)), dma((2, NZ - 1)), dma((2, NZ, NX - 1)),
        dma((2, NZ)), dma((2, NZ)),
    ]
    return pl.pallas_call(
        kernel,
        out_shape=jax.ShapeDtypeStruct((PAIRS, WIDTH), BF16),
        in_specs=[smem] * 4 + [vmem] * 2 + [hbm] * 9,
        out_specs=vmem,
        scratch_shapes=[
            pltpu.VMEM((2, NZ, NX, KEYS, WIDTH), BF16),
            pltpu.VMEM((2, NZ, NX, KEYS, WIDTH), BF16),
            pltpu.VMEM((NT, CMP * TOK, WIDTH), BF16),
            pltpu.VMEM((NT, WIDTH, D), BF16),
            pltpu.VMEM((KEYS, D), BF16),
            pltpu.VMEM((D, WIDTH), BF16),
            pltpu.VMEM((D, WIDTH), BF16),
            pltpu.VMEM((D, WIDTH), BF16),
            pltpu.VMEM((D, FFN), BF16),
            pltpu.VMEM((D, FFN), BF16),
            pltpu.VMEM((FFN, D), BF16),
            pltpu.VMEM((CMP, WIDTH, WIDTH), BF16),
            pltpu.VMEM((CMP, 1, WIDTH), F32),
            pltpu.VMEM((16, D), F32),
            pltpu.VMEM((BATCH, KEYS, WIDTH), F32),
            pltpu.VMEM((BATCH, KEYS, WIDTH), BF16),
            pltpu.VMEM((PAIRS, 16, KEYS), BF16),
            pltpu.VMEM((NT, PAIRS, WIDTH), BF16),
            pltpu.VMEM((NT, PAIRS, WIDTH), F32),
            pltpu.VMEM((NT, PAIRS, WIDTH), BF16),
            pltpu.VMEM((NT, PAIRS, WIDTH), BF16),
            dma((9,)),
        ]
        + gather_sems
        + gather_sems
        + [dma((2, 2, 2, 4)), dma((2, 2, 2, 4)), dma((2, 7)), dma((2, 7)), dma((2, 7))],
        compiler_params=pltpu.CompilerParams(
            collective_id=0, has_side_effects=True, vmem_limit_bytes=48 << 20
        ),
        name="conformer_attention",
    )(
        token_count, pair_compound, pair_conformer.reshape(-1), owner, pair_compound,
        norm_gain.reshape(1, -1), compound_tokens, pocket_tokens, w_query, w_key, w_value,
        w_out, w_gate, w_up, w_down,
    )


def solution(mesh):
    return jax.shard_map(
        local,
        mesh=mesh,
        in_specs=(
            P("pocket", "tensor"),
            P("pocket", None),
            P("pocket"),
            P("pocket", None),
            P("pocket", None),
            P(),
            P(None, "tensor"),
            P(None, "tensor"),
            P(None, "tensor"),
            P("tensor", None),
            P(),
            P(None, "tensor"),
            P(None, "tensor"),
            P("tensor", None),
        ),
        out_specs=P("pocket", "tensor"),
        check_vma=False,
    )
```

```python
import jax
import jax.numpy as jnp
from jax import lax
from jax.experimental import pallas as pl
from jax.experimental.pallas import tpu as pltpu
from jax.sharding import PartitionSpec as P

MESH = pl.DeviceIdType.MESH
NX, NZ, NT = 4, 8, 8
HEAD_DIM = 64
CMP, TOK, KEYS, WIDTH, PAIRS = 8, 64, 256, 128, 128
D, FFN = 1024, 512
SPLIT = 112
VALUES_LATER = 3
BATCH = 16
LOG2E = 1.4426950408889634
F32, BF16 = jnp.float32, jnp.bfloat16
NT_DIMS = (((1,), (1,)), ((), ()))


class Place:
    def __init__(self):
        p = lax.axis_index("pocket")
        self.y = lax.axis_index("tensor")
        self.c = lax.rem(p, 2)
        chip = lax.div(p, 2)
        self.z = lax.rem(chip, NZ)
        self.x = lax.div(chip, NZ)
        self.d = 1 - 2 * self.c
        self.next_x = self.pocket(self.at_x(-1), self.z)
        self.prev_x = self.pocket(self.at_x(1), self.z)
        self.next_z = self.pocket(self.x, self.at_z(-1))
        self.prev_z = self.pocket(self.x, self.at_z(1))
        self.sibling = p + self.d

    def pocket(self, x, z):
        return (x * NZ + z) * 2 + self.c

    def at_x(self, i):
        return lax.rem(self.x - i * self.d + 2 * NX, NX)

    def at_z(self, j):
        return lax.rem(self.z - j * self.d + 2 * NZ, NZ)

    def at_y(self, s):
        return lax.rem(self.y + s + 2 * NT, NT)


class Gather:
    X_OFFSETS = ((0, 1), (1, 2), (-1, 2), (2, 3))
    Z_OFFSETS = (0, 1, -1, 2, -2, 3, -3, 4)

    def __init__(self, at, buf, sems):
        self.at, self.buf = at, buf
        self.ax, self.az, self.bz, self.bx, self.sa, self.sb = sems

    def copy(self, ref, pair, index, pocket):
        return pltpu.make_async_remote_copy(
            src_ref=ref,
            dst_ref=ref,
            send_sem=pair.at[(0,) + index],
            recv_sem=pair.at[(1,) + index],
            device_id=(pocket, self.at.y),
            device_id_type=MESH,
        )

    def block(self, rows, j, i):
        return self.buf.at[self.at.c, self.at.at_z(j), self.at.at_x(i), rows]

    @staticmethod
    def before(o):
        return o - 1 if o > 0 else o + 1

    def along_x(self, rows, pair, j, o, arrived, index):
        return self.copy(
            self.block(rows, j, o if arrived else self.before(o)), pair, index + (o % NX,),
            self.at.next_x if o > 0 else self.at.prev_x,
        )

    def along_z(self, rows, pair, o, i, arrived, index):
        return self.copy(
            self.block(rows, o if arrived else self.before(o), i), pair, index + (o % NZ,),
            self.at.next_z if o > 0 else self.at.prev_z,
        )

    LOW, HIGH = slice(0, SPLIT), slice(SPLIT, KEYS)

    def low_x(self, o, arrived=False):
        return self.along_x(self.LOW, self.ax, 0, o, arrived, ())

    def low_z(self, k, o, arrived=False):
        return self.along_z(self.LOW, self.az, o, k, arrived, (k % NX,))

    def high_z(self, o, arrived=False):
        return self.along_z(self.HIGH, self.bz, o, 0, arrived, ())

    def high_x(self, j, o, arrived=False):
        return self.along_x(self.HIGH, self.bx, j, o, arrived, (j % NZ,))

    def over(self, rows, pair, j, arrived):
        c = 1 - self.at.c if arrived else self.at.c
        z = self.at.at_z(-j) if arrived else self.at.at_z(j)
        return self.copy(self.buf.at[c, z, :, rows], pair, (j % NZ,), self.at.sibling)

    def over_low(self, j, arrived=False):
        return self.over(self.LOW, self.sa, j, arrived)

    def over_high(self, j, arrived=False):
        return self.over(self.HIGH, self.sb, j, arrived)

    def round(self, t):
        if t == 2:
            self.low_x(1, True).wait_recv()
            self.low_x(2).start()
            self.low_x(-1, True).wait_recv()
        if t == 1:
            self.low_x(1).start()
            self.low_x(-1).start()
        if t == 3:
            self.low_x(2, True).wait_recv()
            self.over_low(0).start()
        for k, first in self.X_OFFSETS:
            r = t - first + 1
            for way, last in ((1, NZ // 2), (-1, NZ // 2 - 1)):
                if 1 < r <= last + 1:
                    self.low_z(k, way * (r - 1), True).wait_recv()
                if 1 <= r <= last:
                    self.low_z(k, way * r).start()
            if first == 3 and r > 1:
                for j in self.Z_OFFSETS:
                    if abs(j) == r - 1:
                        self.over_low(j).start()
        for way, last in ((1, NZ // 2), (-1, NZ // 2 - 1)):
            if 1 < t <= last + 1:
                self.high_z(way * (t - 1), True).wait_recv()
            if t <= last:
                self.high_z(way * t).start()
        for j in self.Z_OFFSETS:
            if t == abs(j) + 1:
                self.high_x(j, 1).start()
                self.high_x(j, -1).start()
            if t == abs(j) + 2:
                self.high_x(j, 1, True).wait_recv()
                self.high_x(j, 2).start()
                self.high_x(j, -1, True).wait_recv()
            if t == abs(j) + 3:
                self.high_x(j, 2, True).wait_recv()
                self.over_high(j).start()

    def sends(self):
        zs, xs = self.Z_OFFSETS[1:], (1, -1, 2)
        out = [self.low_x(o) for o in xs]
        out += [self.low_z(k, o) for k, _ in self.X_OFFSETS for o in zs]
        out += [self.high_z(o) for o in zs]
        out += [self.high_x(j, o) for j in self.Z_OFFSETS for o in xs]
        out += [self.over_low(j) for j in self.Z_OFFSETS]
        return out + [self.over_high(j) for j in self.Z_OFFSETS]

    def finish(self):
        for j in self.Z_OFFSETS:
            self.over_low(j, True).wait_recv()
            self.over_high(j, True).wait_recv()


class Ring:
    LAST = ((4, 3), (3, 4))

    def __init__(self, at, piece, sems):
        self.at, self.piece, self.sems = at, piece, sems

    def copy(self, half, way, s, arrived=False):
        hop = s if arrived else s - 1
        ref = self.piece(self.at.at_y(-hop if way == 0 else hop), half)
        return pltpu.make_async_remote_copy(
            src_ref=ref,
            dst_ref=ref,
            send_sem=self.sems.at[0, half, way, s - 1],
            recv_sem=self.sems.at[1, half, way, s - 1],
            device_id=(lax.axis_index("pocket"), self.at.at_y(1 if way == 0 else -1)),
            device_id_type=MESH,
        )

    def step(self, s, half):
        for way in range(2):
            if 1 < s <= self.LAST[half][way] + 1:
                self.copy(half, way, s - 1, True).wait_recv()
            if s <= self.LAST[half][way]:
                self.copy(half, way, s).start()

    def sends(self):
        return [
            self.copy(half, way, s)
            for half in range(2)
            for way in range(2)
            for s in range(1, self.LAST[half][way] + 1)
        ]


def kernel(
    count_s, comp_s, conf_s, owner_s, comp_v, gain_v,
    x_hbm, pt_hbm, wq_hbm, wk_hbm, wv_hbm, wo_hbm, wg_hbm, wu_hbm, wd_hbm,
    out_ref,
    kbuf, vbuf, xbuf, wbuf, pt, wq, wk, wv, wg, wu, wd,
    qt, wt, xm, score, expo, pp, pg, mixed_ref, ds, rs,
    load_sem, k_ax, k_az, k_bz, k_bx, k_sa, k_sb, v_ax, v_az, v_bz, v_bx, v_sa, v_sb,
    x_sem, w_sem, ws_sem, g_sem, r_sem,
):
    at = Place()
    y = at.y
    p = lax.axis_index("pocket")

    def load(i, src, dst):
        copy = pltpu.make_async_copy(src, dst, load_sem.at[i])
        copy.start()
        return copy

    l_pt = load(0, pt_hbm, pt)
    l_wk = load(1, wk_hbm, wk)
    l_x = load(2, x_hbm, xbuf.at[y])
    l_wv = load(3, wv_hbm, wv)
    l_wq = load(4, wq_hbm, wq)
    l_wo = load(5, wo_hbm, wbuf.at[y])
    l_wg = load(6, wg_hbm, wg)
    l_wu = load(7, wu_hbm, wu)
    l_wd = load(8, wd_hbm, wd)

    barrier = pltpu.get_barrier_semaphore()
    for pocket in (at.next_x, at.prev_x, at.next_z, at.prev_z, at.sibling):
        pl.semaphore_signal(barrier, inc=1, device_id=(pocket, y), device_id_type=MESH)
    for s in range(1, NT):
        pl.semaphore_signal(barrier, inc=1, device_id=(p, at.at_y(s)), device_id_type=MESH)

    gk = Gather(at, kbuf, (k_ax, k_az, k_bz, k_bx, k_sa, k_sb))
    gv = Gather(at, vbuf, (v_ax, v_az, v_bz, v_bx, v_sa, v_sb))
    rx = Ring(at, lambda t, half: xbuf.at[t, pl.ds(half * 256, 256)], x_sem)
    rw = Ring(at, lambda t, half: wbuf.at[t, pl.ds(at.c * 64 + half * 32, 32)], w_sem)

    def hand_w(t, i):
        ref = wbuf.at[t, pl.ds(at.c * 64, 64)]
        return pltpu.make_async_remote_copy(
            src_ref=ref, dst_ref=ref, send_sem=ws_sem.at[0, i], recv_sem=ws_sem.at[1, i],
            device_id=(at.sibling, y), device_id_type=MESH,
        )

    def hand_w_arrived(t, i):
        ref = wbuf.at[t, pl.ds((1 - at.c) * 64, 64)]
        return pltpu.make_async_remote_copy(
            src_ref=ref, dst_ref=ref, send_sem=ws_sem.at[0, i], recv_sem=ws_sem.at[1, i],
            device_id=(at.sibling, y), device_id_type=MESH,
        )

    l_pt.wait()
    l_wk.wait()
    kbuf[at.c, at.z, at.x] = jnp.dot(pt[...], wk[...], preferred_element_type=F32).astype(BF16)
    l_x.wait()
    l_wv.wait()
    vbuf[at.c, at.z, at.x] = jnp.dot(pt[...], wv[...], preferred_element_type=F32).astype(BF16)
    pl.semaphore_wait(barrier, 5 + NT - 1)
    for t in range(1, 7):
        if t <= 5:
            rx.step(t, 0)
        gk.round(t)
        if t <= 5:
            rx.step(t, 1)
        if t > VALUES_LATER:
            gv.round(t - VALUES_LATER)

    l_wo.wait()
    rw.step(1, 0)
    rw.step(1, 1)
    l_wq.wait()
    lane = lax.broadcasted_iota(jnp.int32, (1, WIDTH), 1)
    lane_tok = lax.rem(lane, HEAD_DIM)
    row_x = lax.broadcasted_iota(jnp.int32, (16, CMP * TOK), 0)
    lane_x = lax.broadcasted_iota(jnp.int32, (16, CMP * TOK), 1)
    row8 = lax.broadcasted_iota(jnp.int32, (16, 1), 0)
    valid = jnp.zeros((16, CMP * TOK), jnp.bool_)
    count_col = jnp.ones((16, 1), F32)
    for c in range(CMP):
        n = count_s[c]
        nf = n.astype(F32)
        wt[c] = jnp.where(lane_tok < n, 1.0 / jnp.full((1, WIDTH), nf), 0.0)
        valid = jnp.logical_or(
            valid,
            jnp.logical_and(row_x == c, jnp.logical_and(lane_x >= c * TOK, lane_x < c * TOK + n)),
        )
        count_col = jnp.where(row8 == c, nf, count_col)
    valid = jnp.where(valid, 1.0, 0.0).astype(BF16)
    q = jnp.zeros((CMP * TOK, WIDTH), F32)
    for t in range(NT):
        q = q + jnp.dot(xbuf[t], wq[pl.ds(t * WIDTH, WIDTH), :], preferred_element_type=F32)
        xm[:, t * WIDTH : (t + 1) * WIDTH] = (
            jnp.dot(valid, xbuf[t], preferred_element_type=F32) / count_col
        )
    q = q * (HEAD_DIM**-0.5 * LOG2E)
    low_lane = lane < HEAD_DIM
    for c in range(CMP):
        one = q[c * TOK : (c + 1) * TOK]
        block = jnp.concatenate(
            [jnp.where(low_lane, one, 0.0), jnp.where(low_lane, 0.0, one)], axis=0
        )
        qt[c] = block.T.astype(BF16)
    gk.round(7)
    gv.round(7 - VALUES_LATER)
    gk.finish()

    own_head = (
        lax.broadcasted_iota(jnp.int32, (16, WIDTH), 1) // HEAD_DIM
        == lax.broadcasted_iota(jnp.int32, (16, WIDTH), 0)
    )

    def block_of(i):
        b = owner_s[conf_s[i]]
        return lax.bitwise_and(b, 1), lax.bitwise_and(lax.shift_right_logical(b, 1), 7), lax.shift_right_logical(b, 4)

    def forward_w(s):
        rw.step(s, 0)
        rw.step(s, 1)
        for i, t in ((2 * s - 4, 1 - s), (2 * s - 3, s - 1)):
            if i < 7:
                hand_w(at.at_y(t), i).start()

    def attend(i, carry):
        for when, act in (
            (0, lambda: gv.round(8 - VALUES_LATER)),
            (2, lambda: forward_w(2)),
            (3, lambda: gv.round(9 - VALUES_LATER)),
            (5, lambda: forward_w(3)),
            (6, lambda: gv.round(10 - VALUES_LATER)),
        ):
            pl.when(i == when)(act)
        peaks, sums = [], []
        for j in range(BATCH):
            c, z, x = block_of(i * BATCH + j)
            s = jnp.dot(kbuf[c, z, x], qt[comp_s[0, i * BATCH + j]], preferred_element_type=F32)
            score[j] = s
            peaks.append(jnp.max(s, axis=0, keepdims=True))
        for j in range(BATCH):
            e = jnp.exp2(score[j] - peaks[j])
            sums.append(jnp.sum(e, axis=0, keepdims=True))
            expo[j] = e.astype(BF16)
        for j in range(BATCH):
            share = wt[comp_s[0, i * BATCH + j]] / sums[j]
            share = jnp.where(own_head, share, 0.0).astype(BF16)
            pp[i * BATCH + j] = lax.dot_general(
                share, expo[j], NT_DIMS, preferred_element_type=F32
            ).astype(BF16)
        return carry

    lax.fori_loop(0, PAIRS // BATCH, attend, 0)
    forward_w(4)
    gv.finish()

    def weigh(i, carry):
        rows = []
        for j in range(BATCH):
            c, z, x = block_of(i * BATCH + j)
            v = jnp.dot(pp[i * BATCH + j], vbuf[c, z, x], preferred_element_type=F32)
            rows.append(jnp.where(low_lane, v[0:1], v[1:2]))
        pg[y, pl.ds(pl.multiple_of(i * BATCH, BATCH), BATCH), :] = jnp.concatenate(
            rows, axis=0
        ).astype(BF16)
        return carry

    lax.fori_loop(0, PAIRS // BATCH, weigh, 0)

    def to_peer(src, dst, sems, s):
        return pltpu.make_async_remote_copy(
            src_ref=src, dst_ref=dst, send_sem=sems.at[0, s - 1], recv_sem=sems.at[1, s - 1],
            device_id=(p, at.at_y(s)), device_id_type=MESH,
        )

    order = (4, 3, 5, 2, 6, 1, 7)
    for s in order:
        to_peer(pg.at[y], pg.at[y], g_sem, s).start()
    forward_w(5)
    for copy in gk.sends() + gv.sends() + rx.sends() + rw.sends():
        copy.wait_send()
    for s in range(1, 5):
        for i, t in ((2 * s - 2, -s), (2 * s - 1, s)):
            if i < 7:
                hand_w(at.at_y(t), i).wait_send()
                hand_w_arrived(at.at_y(t), i).wait_recv()
    hot = (lax.broadcasted_iota(jnp.int32, (WIDTH, PAIRS), 0) == comp_v[...]).astype(F32).T
    table = jnp.concatenate([xm[0:CMP], jnp.zeros((WIDTH - CMP, D), F32)], axis=0)
    x_pair = jnp.dot(hot, table, precision=lax.Precision.HIGHEST, preferred_element_type=F32)
    l_wg.wait()
    l_wu.wait()
    l_wd.wait()
    for s in range(1, NT):
        to_peer(pg.at[y], pg.at[at.at_y(-s)], g_sem, s).wait_recv()
    mixed = x_pair
    for t in range(NT):
        mixed = mixed + jnp.dot(pg[t], wbuf[t], preferred_element_type=F32)
    for t in range(NT):
        mixed_ref[t] = mixed[:, t * WIDTH : (t + 1) * WIDTH]
    scale = lax.rsqrt(jnp.mean(mixed * mixed, axis=1, keepdims=True) + 1e-05)
    normed = (mixed * scale * gain_v[...]).astype(BF16)
    gate = jnp.dot(normed, wg[...], preferred_element_type=F32)
    up = jnp.dot(normed, wu[...], preferred_element_type=F32)
    hidden = (gate / (1.0 + jnp.exp(-gate)) * up).astype(BF16)

    def share_of(t):
        columns = pl.ds(pl.multiple_of(t * WIDTH, WIDTH), WIDTH)
        return jnp.dot(hidden, wd[:, columns], preferred_element_type=F32)

    for s in order:
        ds[at.at_y(s)] = share_of(at.at_y(s)).astype(BF16)
        to_peer(ds.at[at.at_y(s)], rs.at[y], r_sem, s).start()
    total = share_of(y)
    for s in order:
        to_peer(pg.at[y], pg.at[y], g_sem, s).wait_send()
    for s in order:
        from_y = at.at_y(-s)
        to_peer(ds.at[from_y], rs.at[from_y], r_sem, s).wait_recv()
        total = total + rs[from_y].astype(F32)
    out_ref[...] = (mixed_ref[y] + total).astype(BF16)
    for s in order:
        to_peer(ds.at[at.at_y(s)], rs.at[y], r_sem, s).wait_send()


def local(
    compound_tokens,
    pocket_tokens,
    token_count,
    pair_compound,
    pair_conformer,
    owner,
    w_query,
    w_key,
    w_value,
    w_out,
    norm_gain,
    w_gate,
    w_up,
    w_down,
):
    smem = pl.BlockSpec(memory_space=pltpu.SMEM)
    vmem = pl.BlockSpec(memory_space=pltpu.VMEM)
    hbm = pl.BlockSpec(memory_space=pltpu.HBM)
    dma = pltpu.SemaphoreType.DMA
    gather_sems = [
        dma((2, NX)), dma((2, NX, NZ)), dma((2, NZ)), dma((2, NZ, NX)),
        dma((2, NZ)), dma((2, NZ)),
    ]
    return pl.pallas_call(
        kernel,
        out_shape=jax.ShapeDtypeStruct((PAIRS, WIDTH), BF16),
        in_specs=[smem] * 4 + [vmem] * 2 + [hbm] * 9,
        out_specs=vmem,
        scratch_shapes=[
            pltpu.VMEM((2, NZ, NX, KEYS, WIDTH), BF16),
            pltpu.VMEM((2, NZ, NX, KEYS, WIDTH), BF16),
            pltpu.VMEM((NT, CMP * TOK, WIDTH), BF16),
            pltpu.VMEM((NT, WIDTH, D), BF16),
            pltpu.VMEM((KEYS, D), BF16),
            pltpu.VMEM((D, WIDTH), BF16),
            pltpu.VMEM((D, WIDTH), BF16),
            pltpu.VMEM((D, WIDTH), BF16),
            pltpu.VMEM((D, FFN), BF16),
            pltpu.VMEM((D, FFN), BF16),
            pltpu.VMEM((FFN, D), BF16),
            pltpu.VMEM((CMP, WIDTH, WIDTH), BF16),
            pltpu.VMEM((CMP, 1, WIDTH), F32),
            pltpu.VMEM((16, D), F32),
            pltpu.VMEM((BATCH, KEYS, WIDTH), F32),
            pltpu.VMEM((BATCH, KEYS, WIDTH), BF16),
            pltpu.VMEM((PAIRS, 16, KEYS), BF16),
            pltpu.VMEM((NT, PAIRS, WIDTH), BF16),
            pltpu.VMEM((NT, PAIRS, WIDTH), F32),
            pltpu.VMEM((NT, PAIRS, WIDTH), BF16),
            pltpu.VMEM((NT, PAIRS, WIDTH), BF16),
            dma((9,)),
        ]
        + gather_sems
        + gather_sems
        + [dma((2, 2, 2, 4)), dma((2, 2, 2, 4)), dma((2, 7)), dma((2, 7)), dma((2, 7))],
        compiler_params=pltpu.CompilerParams(
            collective_id=0, has_side_effects=True, vmem_limit_bytes=62 << 20
        ),
        name="conformer_attention",
    )(
        token_count, pair_compound, pair_conformer.reshape(-1), owner, pair_compound,
        norm_gain.reshape(1, -1), compound_tokens, pocket_tokens, w_query, w_key, w_value,
        w_out, w_gate, w_up, w_down,
    )


def solution(mesh):
    return jax.shard_map(
        local,
        mesh=mesh,
        in_specs=(
            P("pocket", "tensor"),
            P("pocket", None),
            P("pocket"),
            P("pocket", None),
            P("pocket", None),
            P(),
            P(None, "tensor"),
            P(None, "tensor"),
            P(None, "tensor"),
            P("tensor", None),
            P(),
            P(None, "tensor"),
            P(None, "tensor"),
            P("tensor", None),
        ),
        out_specs=P("pocket", "tensor"),
        check_vma=False,
    )
```

```python
import heapq

import jax
import jax.numpy as jnp
from jax import lax
from jax.experimental import pallas as pl
from jax.experimental.pallas import tpu as pltpu
from jax.sharding import PartitionSpec as P

MESH = pl.DeviceIdType.MESH
NX, NZ, NT = 4, 8, 8
HEAD_DIM = 64
CMP, TOK, KEYS, WIDTH, PAIRS = 8, 64, 256, 128, 128
D, FFN = 1024, 512
SPLIT = 96
BATCH = 16
PARTS = 2
LOG2E = 1.4426950408889634
F32, BF16 = jnp.float32, jnp.bfloat16
NT_DIMS = (((1,), (1,)), ((), ()))


class Place:
    def __init__(self):
        p = lax.axis_index("pocket")
        self.y = lax.axis_index("tensor")
        self.c = lax.rem(p, 2)
        chip = lax.div(p, 2)
        self.z = lax.rem(chip, NZ)
        self.x = lax.div(chip, NZ)
        self.d = 1 - 2 * self.c
        self.sibling = p + self.d
        self.xs = [lax.rem(self.x - i * self.d + 2 * NX, NX) for i in range(NX)]
        self.zs = [lax.rem(self.z - j * self.d + 2 * NZ, NZ) for j in range(NZ)]
        self.ys = [lax.rem(self.y + s, NT) for s in range(NT)]
        self.x_pockets = [self.pocket(x, self.z) for x in self.xs]
        self.z_pockets = [self.pocket(self.x, z) for z in self.zs]

    def pocket(self, x, z):
        return (x * NZ + z) * 2 + self.c

    def x_off(self, o):
        return self.x_pockets[-o % NX]

    def z_off(self, o):
        return self.z_pockets[-o % NZ]

    def at_x(self, i):
        return self.xs[i % NX]

    def at_z(self, j):
        return self.zs[j % NZ]

    def at_y(self, s):
        return self.ys[s % NT]


Z_LOW = {1: 0, -1: 0, 2: 1, -2: -1, 3: 2, -3: -2, 4: 3}
Z_HIGH = {1: 0, -1: 0, 2: 0, -2: 0, 3: 2, -3: -2, 4: 3}
X_LOW = {1: 0, -1: 0, 2: 0}
X_HIGH = {1: 0, -1: 0, 2: 1}
RING_LAST = ((4, 3), (3, 4))
START_US = {"k": 0.0, "v": 10.0, "x": 0.0, "w": 12.0}
LINK_US = 1 / 100e3
HOP_US, LATENCY_US, ISSUE_US, QUERY_US, STEP_US = 0.5, 3.0, 0.03, 1.0, 1.2


def messages():
    out = {}
    low, high = SPLIT * WIDTH * 2, (KEYS - SPLIT) * WIDTH * 2
    for g in "kv":
        for o, f in X_LOW.items():
            out[g, "lx", o] = "x", abs(o - f), low, (g, "lx", f) if f else None
        for k in (0, 1, -1, 2):
            for o, f in Z_LOW.items():
                first = (g, "lx", k) if k else None
                out[g, "lz", k, o] = "z", abs(o - f), low, (g, "lz", k, f) if f else first
        for o, f in Z_HIGH.items():
            out[g, "hz", o] = "z", abs(o - f), high, (g, "hz", f) if f else None
        for j in (0, *Z_HIGH):
            for o, f in X_HIGH.items():
                first = (g, "hz", j) if j else None
                out[g, "hx", j, o] = "x", abs(o - f), high, (g, "hx", j, f) if f else first
    for g in "xw":
        for half in range(2):
            for way in range(2):
                for r in range(1, RING_LAST[half][way] + 1):
                    out[g, "r", half, way, r] = (
                        "y", 1, 65536, (g, "r", half, way, r - 1) if r > 1 else None
                    )
    return out


def handed(m):
    if m[0] == "w":
        _, _, _, way, r = m
        return "w", "w", r if way == 0 or r == 4 else -r
    if m[0] in "kv" and m[1] != "hz":
        j = {"lx": 0, "lz": m[-1], "hx": m[2]}[m[1]]
        return m[0], m[1][0], j
    return None


def plan():
    every = messages()
    after, depth = {}, {}
    for m, v in every.items():
        after.setdefault(v[3], []).append(m)

    def steps(m):
        if m not in depth:
            depth[m] = 1 + max([steps(n) for n in after.get(m, [])], default=0)
        return depth[m]

    def in_turn(ms):
        return sorted(ms, key=lambda m: (START_US[m[0]], -steps(m), -abs(m[-1])))

    free, queue, ops, now, missing = {}, [], [], 0.0, {}
    for n, m in enumerate(in_turn(after[None])):
        heapq.heappush(queue, (START_US[m[0]], 0, n, "s", m))
    tokens = sum(m[0] == "x" for m in every)

    def send(m):
        link, hops, size, _ = every[m]
        at = now
        for _ in range(hops):
            begin = max(at, free.get(link, 0.0))
            free[link] = begin + size * LINK_US
            at = begin + HOP_US
        heapq.heappush(queue, (at + size * LINK_US + LATENCY_US, 1, len(ops), "w", m))

    while queue:
        at, _, _, kind, m = heapq.heappop(queue)
        now = max(now, at) + ISSUE_US
        ops.append((kind, m, now))
        if kind == "s":
            send(m)
            continue
        for n in in_turn(after.get(m, [])):
            now += ISSUE_US
            ops.append(("s", n, now))
            send(n)
        key = handed(m)
        if key:
            missing[key] = missing.get(key, 2 if m[0] == "w" else 3 if m[1][1] == "x" else 4) - 1
            if not missing[key]:
                now += ISSUE_US
                ops.append(("o", key, now))
        if m[0] == "x":
            tokens -= 1
            if not tokens:
                ops.append(("q", ("q",), now))
                now += QUERY_US
    return ops


class Gather:
    LOW, HIGH = slice(0, SPLIT), slice(SPLIT, KEYS)
    OFFSETS = (0, *Z_HIGH)

    def __init__(self, at, buf, sems):
        self.at, self.buf = at, buf
        self.ax, self.az, self.bz, self.bx, self.sa, self.sb = sems

    def copy(self, ref, pair, index, pocket):
        return pltpu.make_async_remote_copy(
            src_ref=ref,
            dst_ref=ref,
            send_sem=pair.at[(0,) + index],
            recv_sem=pair.at[(1,) + index],
            device_id=(pocket, self.at.y),
            device_id_type=MESH,
        )

    def block(self, rows, j, i):
        return self.buf.at[self.at.c, self.at.at_z(j), self.at.at_x(i), rows]

    def message(self, kind, *index, arrived=False):
        o = index[-1]
        if kind == "lx":
            before, rows, pair, place = X_LOW[o], self.LOW, self.ax, (o % NX,)
        elif kind == "lz":
            before, rows, pair, place = Z_LOW[o], self.LOW, self.az, (index[0] % NX, o % NZ)
        elif kind == "hz":
            before, rows, pair, place = Z_HIGH[o], self.HIGH, self.bz, (o % NZ,)
        else:
            before, rows, pair, place = X_HIGH[o], self.HIGH, self.bx, (index[0] % NZ, o % NX)
        here = o if arrived else before
        if kind[1] == "x":
            ref = self.block(rows, index[0] if kind == "hx" else 0, here)
            return self.copy(ref, pair, place, self.at.x_off(o - before))
        ref = self.block(rows, here, index[0] if kind == "lz" else 0)
        return self.copy(ref, pair, place, self.at.z_off(o - before))

    def over(self, rows, pair, j, arrived):
        c = 1 - self.at.c if arrived else self.at.c
        z = self.at.at_z(-j) if arrived else self.at.at_z(j)
        return self.copy(self.buf.at[c, z, :, rows], pair, (j % NZ,), self.at.sibling)

    def over_low(self, j, arrived=False):
        return self.over(self.LOW, self.sa, j, arrived)

    def over_high(self, j, arrived=False):
        return self.over(self.HIGH, self.sb, j, arrived)

    def hand_overs(self, arrived):
        return [over(j, arrived) for j in self.OFFSETS for over in (self.over_low, self.over_high)]


class Ring:
    def __init__(self, at, piece, sems):
        self.at, self.piece, self.sems = at, piece, sems

    def message(self, kind, half, way, s, arrived=False):
        hop = s if arrived else s - 1
        ref = self.piece(self.at.at_y(-hop if way == 0 else hop), half)
        return pltpu.make_async_remote_copy(
            src_ref=ref,
            dst_ref=ref,
            send_sem=self.sems.at[0, half, way, s - 1],
            recv_sem=self.sems.at[1, half, way, s - 1],
            device_id=(lax.axis_index("pocket"), self.at.at_y(1 if way == 0 else -1)),
            device_id_type=MESH,
        )


def kernel(
    count_s, comp_s, conf_s, owner_s, comp_v, gain_v,
    x_hbm, pt_hbm, wq_hbm, wk_hbm, wv_hbm, wo_hbm, wg_hbm, wu_hbm, wd_hbm,
    out_ref,
    kbuf, vbuf, xbuf, wbuf, pt, wq, wk, wv, wg, wu, wd,
    qt, wt, xm, score, expo, pp, pg, mixed_ref, ds, rs,
    load_sem, k_ax, k_az, k_bz, k_bx, k_sa, k_sb, v_ax, v_az, v_bz, v_bx, v_sa, v_sb,
    x_sem, w_sem, ws_sem, g_sem, r_sem,
):
    at = Place()
    y = at.y
    p = lax.axis_index("pocket")

    def load(i, src, dst):
        copy = pltpu.make_async_copy(src, dst, load_sem.at[i])
        copy.start()
        return copy

    l_pt = load(0, pt_hbm, pt)
    l_wk = load(1, wk_hbm, wk)
    l_x = load(2, x_hbm, xbuf.at[y])
    l_wv = load(3, wv_hbm, wv)
    l_wq = load(4, wq_hbm, wq)

    barrier = pltpu.get_barrier_semaphore()
    near = [at.x_off(o) for o in (1, -1, 2)] + [at.z_off(o) for o in (1, -1, 2, -2)]
    for pocket in near + [at.sibling]:
        pl.semaphore_signal(barrier, inc=1, device_id=(pocket, y), device_id_type=MESH)
    for s in range(1, NT):
        pl.semaphore_signal(barrier, inc=1, device_id=(p, at.at_y(s)), device_id_type=MESH)

    gk = Gather(at, kbuf, (k_ax, k_az, k_bz, k_bx, k_sa, k_sb))
    gv = Gather(at, vbuf, (v_ax, v_az, v_bz, v_bx, v_sa, v_sb))
    rx = Ring(at, lambda t, half: xbuf.at[t, pl.ds(half * 256, 256)], x_sem)
    rw = Ring(at, lambda t, half: wbuf.at[t, pl.ds(at.c * 64 + half * 32, 32)], w_sem)

    def hand_w(o, core):
        ref = wbuf.at[at.at_y(-o), pl.ds(core * 64, 64)]
        return pltpu.make_async_remote_copy(
            src_ref=ref, dst_ref=ref, send_sem=ws_sem.at[0, o % NT], recv_sem=ws_sem.at[1, o % NT],
            device_id=(at.sibling, y), device_id_type=MESH,
        )

    flows = {"k": gk, "v": gv, "x": rx, "w": rw}

    def act(kind, m):
        flow = flows[m[0]]
        if kind == "s":
            flow.message(*m[1:]).start()
        elif kind == "w":
            flow.message(*m[1:], arrived=True).wait_recv()
        elif m[0] == "w":
            hand_w(m[2], at.c).start()
        else:
            (flow.over_low if m[1] == "l" else flow.over_high)(m[2]).start()

    ops = plan()
    keys_end = max(n for n, (_, m, _) in enumerate(ops) if m[0] == "k") + 1

    l_pt.wait()
    l_wk.wait()
    kbuf[at.c, at.z, at.x] = jnp.dot(pt[...], wk[...], preferred_element_type=F32).astype(BF16)
    l_x.wait()
    pl.semaphore_wait(barrier, 8 + NT - 1)
    l_wo = load(5, wo_hbm, wbuf.at[y])
    l_wg = load(6, wg_hbm, wg)
    l_wu = load(7, wu_hbm, wu)
    l_wd = load(8, wd_hbm, wd)

    lane = lax.broadcasted_iota(jnp.int32, (1, WIDTH), 1)
    low_lane = lane < HEAD_DIM

    def make_queries():
        lane_tok = lax.rem(lane, HEAD_DIM)
        row_x = lax.broadcasted_iota(jnp.int32, (16, CMP * TOK), 0)
        lane_x = lax.broadcasted_iota(jnp.int32, (16, CMP * TOK), 1)
        row8 = lax.broadcasted_iota(jnp.int32, (16, 1), 0)
        valid = jnp.zeros((16, CMP * TOK), jnp.bool_)
        count_col = jnp.ones((16, 1), F32)
        for c in range(CMP):
            n = count_s[c]
            nf = n.astype(F32)
            wt[c] = jnp.where(lane_tok < n, 1.0 / jnp.full((1, WIDTH), nf), 0.0)
            valid = jnp.logical_or(
                valid,
                jnp.logical_and(row_x == c, jnp.logical_and(lane_x >= c * TOK, lane_x < c * TOK + n)),
            )
            count_col = jnp.where(row8 == c, nf, count_col)
        valid = jnp.where(valid, 1.0, 0.0).astype(BF16)
        q = jnp.zeros((CMP * TOK, WIDTH), F32)
        for t in range(NT):
            q = q + jnp.dot(xbuf[t], wq[pl.ds(t * WIDTH, WIDTH), :], preferred_element_type=F32)
            xm[:, t * WIDTH : (t + 1) * WIDTH] = (
                jnp.dot(valid, xbuf[t], preferred_element_type=F32) / count_col
            )
        q = q * (HEAD_DIM**-0.5 * LOG2E)
        for c in range(CMP):
            one = q[c * TOK : (c + 1) * TOK]
            block = jnp.concatenate(
                [jnp.where(low_lane, one, 0.0), jnp.where(low_lane, 0.0, one)], axis=0
            )
            qt[c] = block.T.astype(BF16)

    values_at = next(n for n, (_, m, _) in enumerate(ops) if m[0] == "v")
    w_at = next(n for n, (_, m, _) in enumerate(ops) if m[0] == "w")
    for n, (kind, m, _) in enumerate(ops[:keys_end]):
        if n == values_at:
            l_wv.wait()
            vbuf[at.c, at.z, at.x] = jnp.dot(
                pt[...], wv[...], preferred_element_type=F32
            ).astype(BF16)
        if n == w_at:
            l_wo.wait()
        if kind == "q":
            l_wq.wait()
            make_queries()
        else:
            act(kind, m)
    assert max(values_at, w_at, [kind for kind, _, _ in ops].index("q")) < keys_end
    for copy in gk.hand_overs(True):
        copy.wait_recv()

    own_head = (
        lax.broadcasted_iota(jnp.int32, (16, WIDTH), 1) // HEAD_DIM
        == lax.broadcasted_iota(jnp.int32, (16, WIDTH), 0)
    )

    def block_of(i):
        b = owner_s[conf_s[i]]
        return lax.bitwise_and(b, 1), lax.bitwise_and(lax.shift_right_logical(b, 1), 7), lax.shift_right_logical(b, 4)

    steps = PAIRS // BATCH
    later = [[] for _ in range(steps + 1)]
    for kind, m, when in ops[keys_end:]:
        later[min(steps, max(0, int((when - ops[keys_end - 1][2]) / STEP_US)))].append((kind, m))

    def go(some):
        for kind, m in some:
            act(kind, m)

    def attend(i, carry):
        for n in range(steps):
            if later[n]:
                pl.when(i == n)(lambda n=n: go(later[n]))
        peaks, sums = [], []
        for j in range(BATCH):
            c, z, x = block_of(i * BATCH + j)
            s = jnp.dot(kbuf[c, z, x], qt[comp_s[0, i * BATCH + j]], preferred_element_type=F32)
            score[j] = s
            peaks.append(jnp.max(s, axis=0, keepdims=True))
        for j in range(BATCH):
            e = jnp.exp2(score[j] - peaks[j])
            sums.append(jnp.sum(e, axis=0, keepdims=True))
            expo[j] = e.astype(BF16)
        for j in range(BATCH):
            share = wt[comp_s[0, i * BATCH + j]] / sums[j]
            share = jnp.where(own_head, share, 0.0).astype(BF16)
            pp[i * BATCH + j] = lax.dot_general(
                share, expo[j], NT_DIMS, preferred_element_type=F32
            ).astype(BF16)
        return carry

    lax.fori_loop(0, PAIRS // BATCH, attend, 0)
    go(later[steps])
    for copy in gv.hand_overs(True):
        copy.wait_recv()

    def weigh(i, carry):
        rows = []
        for j in range(BATCH):
            c, z, x = block_of(i * BATCH + j)
            v = jnp.dot(pp[i * BATCH + j], vbuf[c, z, x], preferred_element_type=F32)
            rows.append(jnp.where(low_lane, v[0:1], v[1:2]))
        pg[y, pl.ds(pl.multiple_of(i * BATCH, BATCH), BATCH), :] = jnp.concatenate(
            rows, axis=0
        ).astype(BF16)
        return carry

    def to_peer(src, dst, sems, n, s):
        return pltpu.make_async_remote_copy(
            src_ref=src, dst_ref=dst,
            send_sem=sems.at[0, n, s - 1], recv_sem=sems.at[1, n, s - 1],
            device_id=(p, at.at_y(s)), device_id_type=MESH,
        )

    order = (4, 3, 5, 2, 6, 1, 7)
    parts = [slice(n * PAIRS // PARTS, (n + 1) * PAIRS // PARTS) for n in range(PARTS)]

    def pooled(n, s):
        return to_peer(pg.at[y, parts[n]], pg.at[y, parts[n]], g_sem, n, s)

    def pooled_came(n, s):
        ref = pg.at[at.at_y(-s), parts[n]]
        return to_peer(ref, ref, g_sem, n, s)

    def share(n, s):
        return to_peer(ds.at[at.at_y(s), parts[n]], rs.at[y, parts[n]], r_sem, n, s)

    def share_came(n, s):
        ref = rs.at[at.at_y(-s), parts[n]]
        return to_peer(ref, ref, r_sem, n, s)

    for n in range(PARTS):
        lax.fori_loop(n * steps // PARTS, (n + 1) * steps // PARTS, weigh, 0)
        for s in order:
            pooled(n, s).start()
    hot = (lax.broadcasted_iota(jnp.int32, (WIDTH, PAIRS), 0) == comp_v[...]).astype(F32).T
    table = jnp.concatenate([xm[0:CMP], jnp.zeros((WIDTH - CMP, D), F32)], axis=0)
    x_pair = jnp.dot(hot, table, precision=lax.Precision.HIGHEST, preferred_element_type=F32)
    l_wg.wait()
    l_wu.wait()
    l_wd.wait()
    for o in (1, -1, 2, -2, 3, -3, 4):
        hand_w(o, 1 - at.c).wait_recv()
    for kind, m, _ in ops:
        if kind == "s":
            flows[m[0]].message(*m[1:]).wait_send()
    for copy in gk.hand_overs(False) + gv.hand_overs(False):
        copy.wait_send()
    for o in (1, -1, 2, -2, 3, -3, 4):
        hand_w(o, at.c).wait_send()
    own = []
    for n in range(PARTS):
        for s in order:
            pooled_came(n, s).wait_recv()
        mixed = x_pair[parts[n]]
        for t in range(NT):
            mixed = mixed + jnp.dot(
                pg[t, parts[n]], wbuf[t], preferred_element_type=F32
            )
        for t in range(NT):
            mixed_ref[t, parts[n]] = mixed[:, t * WIDTH : (t + 1) * WIDTH]
        scale = lax.rsqrt(jnp.mean(mixed * mixed, axis=1, keepdims=True) + 1e-05)
        normed = (mixed * scale * gain_v[...]).astype(BF16)
        gate = jnp.dot(normed, wg[...], preferred_element_type=F32)
        up = jnp.dot(normed, wu[...], preferred_element_type=F32)
        hidden = (gate / (1.0 + jnp.exp(-gate)) * up).astype(BF16)

        def share_of(t):
            columns = pl.ds(pl.multiple_of(t * WIDTH, WIDTH), WIDTH)
            return jnp.dot(hidden, wd[:, columns], preferred_element_type=F32)

        for s in order:
            ds[at.at_y(s), parts[n]] = share_of(at.at_y(s)).astype(BF16)
            share(n, s).start()
        own.append(share_of(y))
    for n in range(PARTS):
        for s in order:
            pooled(n, s).wait_send()
    for n in range(PARTS):
        total = own[n]
        for s in order:
            share_came(n, s).wait_recv()
            total = total + rs[at.at_y(-s), parts[n]].astype(F32)
        out_ref[parts[n]] = (mixed_ref[y, parts[n]] + total).astype(BF16)
    for n in range(PARTS):
        for s in order:
            share(n, s).wait_send()


def local(
    compound_tokens,
    pocket_tokens,
    token_count,
    pair_compound,
    pair_conformer,
    owner,
    w_query,
    w_key,
    w_value,
    w_out,
    norm_gain,
    w_gate,
    w_up,
    w_down,
):
    smem = pl.BlockSpec(memory_space=pltpu.SMEM)
    vmem = pl.BlockSpec(memory_space=pltpu.VMEM)
    hbm = pl.BlockSpec(memory_space=pltpu.HBM)
    dma = pltpu.SemaphoreType.DMA
    gather_sems = [
        dma((2, NX)), dma((2, NX, NZ)), dma((2, NZ)), dma((2, NZ, NX)),
        dma((2, NZ)), dma((2, NZ)),
    ]
    return pl.pallas_call(
        kernel,
        out_shape=jax.ShapeDtypeStruct((PAIRS, WIDTH), BF16),
        in_specs=[smem] * 4 + [vmem] * 2 + [hbm] * 9,
        out_specs=vmem,
        scratch_shapes=[
            pltpu.VMEM((2, NZ, NX, KEYS, WIDTH), BF16),
            pltpu.VMEM((2, NZ, NX, KEYS, WIDTH), BF16),
            pltpu.VMEM((NT, CMP * TOK, WIDTH), BF16),
            pltpu.VMEM((NT, WIDTH, D), BF16),
            pltpu.VMEM((KEYS, D), BF16),
            pltpu.VMEM((D, WIDTH), BF16),
            pltpu.VMEM((D, WIDTH), BF16),
            pltpu.VMEM((D, WIDTH), BF16),
            pltpu.VMEM((D, FFN), BF16),
            pltpu.VMEM((D, FFN), BF16),
            pltpu.VMEM((FFN, D), BF16),
            pltpu.VMEM((CMP, WIDTH, WIDTH), BF16),
            pltpu.VMEM((CMP, 1, WIDTH), F32),
            pltpu.VMEM((16, D), F32),
            pltpu.VMEM((BATCH, KEYS, WIDTH), F32),
            pltpu.VMEM((BATCH, KEYS, WIDTH), BF16),
            pltpu.VMEM((PAIRS, 16, KEYS), BF16),
            pltpu.VMEM((NT, PAIRS, WIDTH), BF16),
            pltpu.VMEM((NT, PAIRS, WIDTH), F32),
            pltpu.VMEM((NT, PAIRS, WIDTH), BF16),
            pltpu.VMEM((NT, PAIRS, WIDTH), BF16),
            dma((9,)),
        ]
        + gather_sems
        + gather_sems
        + [dma((2, 2, 2, 4)), dma((2, 2, 2, 4)), dma((2, NT)), dma((2, PARTS, 7)), dma((2, PARTS, 7))],
        compiler_params=pltpu.CompilerParams(
            collective_id=0, has_side_effects=True, vmem_limit_bytes=62 << 20
        ),
        name="conformer_attention",
    )(
        token_count, pair_compound, pair_conformer.reshape(-1), owner, pair_compound,
        norm_gain.reshape(1, -1), compound_tokens, pocket_tokens, w_query, w_key, w_value,
        w_out, w_gate, w_up, w_down,
    )


def solution(mesh):
    return jax.shard_map(
        local,
        mesh=mesh,
        in_specs=(
            P("pocket", "tensor"),
            P("pocket", None),
            P("pocket"),
            P("pocket", None),
            P("pocket", None),
            P(),
            P(None, "tensor"),
            P(None, "tensor"),
            P(None, "tensor"),
            P("tensor", None),
            P(),
            P(None, "tensor"),
            P(None, "tensor"),
            P("tensor", None),
        ),
        out_specs=P("pocket", "tensor"),
        check_vma=False,
    )
```

```python
import heapq

import jax
import jax.numpy as jnp
from jax import lax
from jax.experimental import pallas as pl
from jax.experimental.pallas import tpu as pltpu
from jax.sharding import PartitionSpec as P

MESH = pl.DeviceIdType.MESH
NX, NZ, NT = 4, 8, 8
HEAD_DIM = 64
CMP, TOK, KEYS, WIDTH, PAIRS = 8, 64, 256, 128, 128
D, FFN = 1024, 512
SPLIT = 96
BATCH = 16
PARTS = 2
LOG2E = 1.4426950408889634
F32, BF16 = jnp.float32, jnp.bfloat16
NT_DIMS = (((1,), (1,)), ((), ()))


class Place:
    def __init__(self):
        p = lax.axis_index("pocket")
        self.y = lax.axis_index("tensor")
        self.c = lax.rem(p, 2)
        chip = lax.div(p, 2)
        self.z = lax.rem(chip, NZ)
        self.x = lax.div(chip, NZ)
        self.d = 1 - 2 * self.c
        self.sibling = p + self.d
        self.xs = [lax.rem(self.x - i * self.d + 2 * NX, NX) for i in range(NX)]
        self.zs = [lax.rem(self.z - j * self.d + 2 * NZ, NZ) for j in range(NZ)]
        self.ys = [lax.rem(self.y + s, NT) for s in range(NT)]
        self.x_pockets = [self.pocket(x, self.z) for x in self.xs]
        self.z_pockets = [self.pocket(self.x, z) for z in self.zs]

    def pocket(self, x, z):
        return (x * NZ + z) * 2 + self.c

    def x_off(self, o):
        return self.x_pockets[-o % NX]

    def z_off(self, o):
        return self.z_pockets[-o % NZ]

    def at_x(self, i):
        return self.xs[i % NX]

    def at_z(self, j):
        return self.zs[j % NZ]

    def at_y(self, s):
        return self.ys[s % NT]


Z_LOW = {1: 0, -1: 0, 2: 1, -2: -1, 3: 2, -3: -2, 4: 3}
Z_HIGH = {1: 0, -1: 0, 2: 0, -2: 0, 3: 2, -3: -2, 4: 3}
X_LOW = {1: 0, -1: 0, 2: 0}
X_HIGH = {1: 0, -1: 0, 2: 1}
RING_LAST = ((4, 3), (3, 4))
START_US = {"k": 0.0, "v": 10.0, "x": 0.0, "w": 12.0}
LINK_US = 1 / 100e3
HOP_US, LATENCY_US, ISSUE_US, QUERY_US, STEP_US = 0.5, 3.0, 0.03, 1.0, 1.2


def messages():
    out = {}
    low, high = SPLIT * WIDTH * 2, (KEYS - SPLIT) * WIDTH * 2
    for g in "kv":
        for o, f in X_LOW.items():
            out[g, "lx", o] = "x", abs(o - f), low, (g, "lx", f) if f else None
        for k in (0, 1, -1, 2):
            for o, f in Z_LOW.items():
                first = (g, "lx", k) if k else None
                out[g, "lz", k, o] = "z", abs(o - f), low, (g, "lz", k, f) if f else first
        for o, f in Z_HIGH.items():
            out[g, "hz", o] = "z", abs(o - f), high, (g, "hz", f) if f else None
        for j in (0, *Z_HIGH):
            for o, f in X_HIGH.items():
                first = (g, "hz", j) if j else None
                out[g, "hx", j, o] = "x", abs(o - f), high, (g, "hx", j, f) if f else first
    for g in "xw":
        for half in range(2):
            for way in range(2):
                for r in range(1, RING_LAST[half][way] + 1):
                    out[g, "r", half, way, r] = (
                        "y", 1, 65536, (g, "r", half, way, r - 1) if r > 1 else None
                    )
    return out


def handed(m):
    if m[0] == "w":
        _, _, _, way, r = m
        return "w", "w", r if way == 0 or r == 4 else -r
    if m[0] in "kv" and m[1] != "hz":
        j = {"lx": 0, "lz": m[-1], "hx": m[2]}[m[1]]
        return m[0], m[1][0], j
    return None


def plan():
    every = messages()
    after, depth = {}, {}
    for m, v in every.items():
        after.setdefault(v[3], []).append(m)

    def steps(m):
        if m not in depth:
            depth[m] = 1 + max([steps(n) for n in after.get(m, [])], default=0)
        return depth[m]

    def in_turn(ms):
        return sorted(ms, key=lambda m: (START_US[m[0]], -steps(m), -abs(m[-1])))

    free, queue, ops, now, missing = {}, [], [], 0.0, {}
    for n, m in enumerate(in_turn(after[None])):
        heapq.heappush(queue, (START_US[m[0]], 0, n, "s", m))
    tokens = sum(m[0] == "x" for m in every)

    def send(m):
        link, hops, size, _ = every[m]
        at = now
        for _ in range(hops):
            begin = max(at, free.get(link, 0.0))
            free[link] = begin + size * LINK_US
            at = begin + HOP_US
        heapq.heappush(queue, (at + size * LINK_US + LATENCY_US, 1, len(ops), "w", m))

    while queue:
        at, _, _, kind, m = heapq.heappop(queue)
        now = max(now, at) + ISSUE_US
        ops.append((kind, m, now))
        if kind == "s":
            send(m)
            continue
        for n in in_turn(after.get(m, [])):
            now += ISSUE_US
            ops.append(("s", n, now))
            send(n)
        key = handed(m)
        if key:
            missing[key] = missing.get(key, 2 if m[0] == "w" else 3 if m[1][1] == "x" else 4) - 1
            if not missing[key]:
                now += ISSUE_US
                ops.append(("o", key, now))
        if m[0] == "x":
            tokens -= 1
            if not tokens:
                ops.append(("q", ("q",), now))
                now += QUERY_US
    return ops


class Gather:
    LOW, HIGH = slice(0, SPLIT), slice(SPLIT, KEYS)
    OFFSETS = (0, *Z_HIGH)

    def __init__(self, at, buf, sems):
        self.at, self.buf = at, buf
        self.ax, self.az, self.bz, self.bx, self.sa, self.sb = sems

    def copy(self, ref, pair, index, pocket):
        return pltpu.make_async_remote_copy(
            src_ref=ref,
            dst_ref=ref,
            send_sem=pair.at[(0,) + index],
            recv_sem=pair.at[(1,) + index],
            device_id=(pocket, self.at.y),
            device_id_type=MESH,
        )

    def block(self, rows, j, i):
        return self.buf.at[self.at.c, self.at.at_z(j), self.at.at_x(i), rows]

    def message(self, kind, *index, arrived=False):
        o = index[-1]
        if kind == "lx":
            before, rows, pair, place = X_LOW[o], self.LOW, self.ax, (o % NX,)
        elif kind == "lz":
            before, rows, pair, place = Z_LOW[o], self.LOW, self.az, (index[0] % NX, o % NZ)
        elif kind == "hz":
            before, rows, pair, place = Z_HIGH[o], self.HIGH, self.bz, (o % NZ,)
        else:
            before, rows, pair, place = X_HIGH[o], self.HIGH, self.bx, (index[0] % NZ, o % NX)
        here = o if arrived else before
        if kind[1] == "x":
            ref = self.block(rows, index[0] if kind == "hx" else 0, here)
            return self.copy(ref, pair, place, self.at.x_off(o - before))
        ref = self.block(rows, here, index[0] if kind == "lz" else 0)
        return self.copy(ref, pair, place, self.at.z_off(o - before))

    def over(self, rows, pair, j, arrived):
        c = 1 - self.at.c if arrived else self.at.c
        z = self.at.at_z(-j) if arrived else self.at.at_z(j)
        return self.copy(self.buf.at[c, z, :, rows], pair, (j % NZ,), self.at.sibling)

    def over_low(self, j, arrived=False):
        return self.over(self.LOW, self.sa, j, arrived)

    def over_high(self, j, arrived=False):
        return self.over(self.HIGH, self.sb, j, arrived)

    def hand_overs(self, arrived):
        return [over(j, arrived) for j in self.OFFSETS for over in (self.over_low, self.over_high)]


class Ring:
    def __init__(self, at, piece, sems):
        self.at, self.piece, self.sems = at, piece, sems

    def message(self, kind, half, way, s, arrived=False):
        hop = s if arrived else s - 1
        ref = self.piece(self.at.at_y(-hop if way == 0 else hop), half)
        return pltpu.make_async_remote_copy(
            src_ref=ref,
            dst_ref=ref,
            send_sem=self.sems.at[0, half, way, s - 1],
            recv_sem=self.sems.at[1, half, way, s - 1],
            device_id=(lax.axis_index("pocket"), self.at.at_y(1 if way == 0 else -1)),
            device_id_type=MESH,
        )


def kernel(
    count_s, comp_s, conf_s, owner_s, comp_v, gain_v,
    x_hbm, pt_hbm, wq_hbm, wk_hbm, wv_hbm, wo_hbm, wg_hbm, wu_hbm, wd_hbm,
    out_ref,
    kbuf, vbuf, xbuf, wbuf, pt, wq, wk, wv, wg, wu, wd,
    qt, wt, xm, score, expo, pp, pg, mixed_ref, ds, rs,
    load_sem, k_ax, k_az, k_bz, k_bx, k_sa, k_sb, v_ax, v_az, v_bz, v_bx, v_sa, v_sb,
    x_sem, w_sem, ws_sem, g_sem, r_sem,
):
    at = Place()
    y = at.y
    p = lax.axis_index("pocket")

    def load(i, src, dst):
        copy = pltpu.make_async_copy(src, dst, load_sem.at[i])
        copy.start()
        return copy

    l_pt = load(0, pt_hbm, pt)
    l_wk = load(1, wk_hbm, wk)
    l_x = load(2, x_hbm, xbuf.at[y])
    l_wv = load(3, wv_hbm, wv)
    l_wq = load(4, wq_hbm, wq)

    barrier = pltpu.get_barrier_semaphore()
    near = [at.x_off(o) for o in (1, -1, 2)] + [at.z_off(o) for o in (1, -1, 2, -2)]
    for pocket in near + [at.sibling]:
        pl.semaphore_signal(barrier, inc=1, device_id=(pocket, y), device_id_type=MESH)
    for s in range(1, NT):
        pl.semaphore_signal(barrier, inc=1, device_id=(p, at.at_y(s)), device_id_type=MESH)

    gk = Gather(at, kbuf, (k_ax, k_az, k_bz, k_bx, k_sa, k_sb))
    gv = Gather(at, vbuf, (v_ax, v_az, v_bz, v_bx, v_sa, v_sb))
    rx = Ring(at, lambda t, half: xbuf.at[t, pl.ds(half * 256, 256)], x_sem)
    rw = Ring(at, lambda t, half: wbuf.at[t, pl.ds(at.c * 64 + half * 32, 32)], w_sem)

    def hand_w(o, core):
        ref = wbuf.at[at.at_y(-o), pl.ds(core * 64, 64)]
        return pltpu.make_async_remote_copy(
            src_ref=ref, dst_ref=ref, send_sem=ws_sem.at[0, o % NT], recv_sem=ws_sem.at[1, o % NT],
            device_id=(at.sibling, y), device_id_type=MESH,
        )

    flows = {"k": gk, "v": gv, "x": rx, "w": rw}

    def act(kind, m):
        flow = flows[m[0]]
        if kind == "s":
            flow.message(*m[1:]).start()
        elif kind == "w":
            flow.message(*m[1:], arrived=True).wait_recv()
        elif m[0] == "w":
            hand_w(m[2], at.c).start()
        else:
            (flow.over_low if m[1] == "l" else flow.over_high)(m[2]).start()

    ops = plan()
    keys_end = max(n for n, (_, m, _) in enumerate(ops) if m[0] == "k") + 1

    l_pt.wait()
    l_wk.wait()
    kbuf[at.c, at.z, at.x] = jnp.dot(pt[...], wk[...], preferred_element_type=F32).astype(BF16)
    l_x.wait()
    pl.semaphore_wait(barrier, 8 + NT - 1)
    l_wo = load(5, wo_hbm, wbuf.at[y])
    l_wg = load(6, wg_hbm, wg)
    l_wu = load(7, wu_hbm, wu)
    l_wd = load(8, wd_hbm, wd)

    lane = lax.broadcasted_iota(jnp.int32, (1, WIDTH), 1)
    low_lane = lane < HEAD_DIM

    def make_queries():
        lane_tok = lax.rem(lane, HEAD_DIM)
        for c in range(CMP):
            n = count_s[c]
            nf = n.astype(F32)
            wt[c] = jnp.where(lane_tok < n, 1.0 / jnp.full((1, WIDTH), nf), 0.0)
        q = jnp.zeros((CMP * TOK, WIDTH), F32)
        for t in range(NT):
            q = q + jnp.dot(xbuf[t], wq[pl.ds(t * WIDTH, WIDTH), :], preferred_element_type=F32)
        q = q * (HEAD_DIM**-0.5 * LOG2E)
        for c in range(CMP):
            one = q[c * TOK : (c + 1) * TOK]
            block = jnp.concatenate(
                [jnp.where(low_lane, one, 0.0), jnp.where(low_lane, 0.0, one)], axis=0
            )
            qt[c] = block.T.astype(BF16)

    values_at = next(n for n, (_, m, _) in enumerate(ops) if m[0] == "v")
    w_at = next(n for n, (_, m, _) in enumerate(ops) if m[0] == "w")
    for n, (kind, m, _) in enumerate(ops[:keys_end]):
        if n == values_at:
            l_wv.wait()
            vbuf[at.c, at.z, at.x] = jnp.dot(
                pt[...], wv[...], preferred_element_type=F32
            ).astype(BF16)
        if n == w_at:
            l_wo.wait()
        if kind == "q":
            l_wq.wait()
            make_queries()
        else:
            act(kind, m)
    assert max(values_at, w_at, [kind for kind, _, _ in ops].index("q")) < keys_end
    for copy in gk.hand_overs(True):
        copy.wait_recv()

    own_head = (
        lax.broadcasted_iota(jnp.int32, (16, WIDTH), 1) // HEAD_DIM
        == lax.broadcasted_iota(jnp.int32, (16, WIDTH), 0)
    )

    def block_of(i):
        b = owner_s[conf_s[i]]
        return lax.bitwise_and(b, 1), lax.bitwise_and(lax.shift_right_logical(b, 1), 7), lax.shift_right_logical(b, 4)

    steps = PAIRS // BATCH
    later = [[] for _ in range(steps + 1)]
    for kind, m, when in ops[keys_end:]:
        later[min(steps, max(0, int((when - ops[keys_end - 1][2]) / STEP_US)))].append((kind, m))

    def go(some):
        for kind, m in some:
            act(kind, m)

    def attend(i, carry):
        for n in range(steps):
            if later[n]:
                pl.when(i == n)(lambda n=n: go(later[n]))
        peaks, sums = [], []
        for j in range(BATCH):
            c, z, x = block_of(i * BATCH + j)
            s = jnp.dot(kbuf[c, z, x], qt[comp_s[0, i * BATCH + j]], preferred_element_type=F32)
            score[j] = s
            peaks.append(jnp.max(s, axis=0, keepdims=True))
        for j in range(BATCH):
            e = jnp.exp2(score[j] - peaks[j])
            sums.append(jnp.sum(e, axis=0, keepdims=True))
            expo[j] = e.astype(BF16)
        for j in range(BATCH):
            share = wt[comp_s[0, i * BATCH + j]] / sums[j]
            share = jnp.where(own_head, share, 0.0).astype(BF16)
            pp[i * BATCH + j] = lax.dot_general(
                share, expo[j], NT_DIMS, preferred_element_type=F32
            ).astype(BF16)
        return carry

    lax.fori_loop(0, PAIRS // BATCH, attend, 0)
    go(later[steps])
    for copy in gv.hand_overs(True):
        copy.wait_recv()

    def weigh(i, carry):
        rows = []
        for j in range(BATCH):
            c, z, x = block_of(i * BATCH + j)
            v = jnp.dot(pp[i * BATCH + j], vbuf[c, z, x], preferred_element_type=F32)
            rows.append(jnp.where(low_lane, v[0:1], v[1:2]))
        pg[y, pl.ds(pl.multiple_of(i * BATCH, BATCH), BATCH), :] = jnp.concatenate(
            rows, axis=0
        ).astype(BF16)
        return carry

    def to_peer(src, dst, sems, n, s):
        return pltpu.make_async_remote_copy(
            src_ref=src, dst_ref=dst,
            send_sem=sems.at[0, n, s - 1], recv_sem=sems.at[1, n, s - 1],
            device_id=(p, at.at_y(s)), device_id_type=MESH,
        )

    order = (4, 3, 5, 2, 6, 1, 7)
    parts = [slice(n * PAIRS // PARTS, (n + 1) * PAIRS // PARTS) for n in range(PARTS)]

    def pooled(n, s):
        return to_peer(pg.at[y, parts[n]], pg.at[y, parts[n]], g_sem, n, s)

    def pooled_came(n, s):
        ref = pg.at[at.at_y(-s), parts[n]]
        return to_peer(ref, ref, g_sem, n, s)

    def share(n, s):
        return to_peer(ds.at[at.at_y(s), parts[n]], rs.at[y, parts[n]], r_sem, n, s)

    def share_came(n, s):
        ref = rs.at[at.at_y(-s), parts[n]]
        return to_peer(ref, ref, r_sem, n, s)

    for n in range(PARTS):
        lax.fori_loop(n * steps // PARTS, (n + 1) * steps // PARTS, weigh, 0)
        for s in order:
            pooled(n, s).start()
    row_x = lax.broadcasted_iota(jnp.int32, (16, CMP * TOK), 0)
    lane_x = lax.broadcasted_iota(jnp.int32, (16, CMP * TOK), 1)
    row8 = lax.broadcasted_iota(jnp.int32, (16, 1), 0)
    valid = jnp.zeros((16, CMP * TOK), jnp.bool_)
    count_col = jnp.ones((16, 1), F32)
    for c in range(CMP):
        n = count_s[c]
        nf = n.astype(F32)
        valid = jnp.logical_or(
            valid,
            jnp.logical_and(row_x == c, jnp.logical_and(lane_x >= c * TOK, lane_x < c * TOK + n)),
        )
        count_col = jnp.where(row8 == c, nf, count_col)
    valid = jnp.where(valid, 1.0, 0.0).astype(BF16)
    for t in range(NT):
        xm[:, t * WIDTH : (t + 1) * WIDTH] = (
            jnp.dot(valid, xbuf[t], preferred_element_type=F32) / count_col
        )
    hot = (lax.broadcasted_iota(jnp.int32, (WIDTH, PAIRS), 0) == comp_v[...]).astype(F32).T
    table = jnp.concatenate([xm[0:CMP], jnp.zeros((WIDTH - CMP, D), F32)], axis=0)
    x_pair = jnp.dot(hot, table, precision=lax.Precision.HIGHEST, preferred_element_type=F32)
    l_wg.wait()
    l_wu.wait()
    l_wd.wait()
    for o in (1, -1, 2, -2, 3, -3, 4):
        hand_w(o, 1 - at.c).wait_recv()
    for kind, m, _ in ops:
        if kind == "s":
            flows[m[0]].message(*m[1:]).wait_send()
    for copy in gk.hand_overs(False) + gv.hand_overs(False):
        copy.wait_send()
    for o in (1, -1, 2, -2, 3, -3, 4):
        hand_w(o, at.c).wait_send()
    own = []
    for n in range(PARTS):
        for s in order:
            pooled_came(n, s).wait_recv()
        mixed = x_pair[parts[n]]
        for t in range(NT):
            mixed = mixed + jnp.dot(
                pg[t, parts[n]], wbuf[t], preferred_element_type=F32
            )
        for t in range(NT):
            mixed_ref[t, parts[n]] = mixed[:, t * WIDTH : (t + 1) * WIDTH]
        scale = lax.rsqrt(jnp.mean(mixed * mixed, axis=1, keepdims=True) + 1e-05)
        normed = (mixed * scale * gain_v[...]).astype(BF16)
        gate = jnp.dot(normed, wg[...], preferred_element_type=F32)
        up = jnp.dot(normed, wu[...], preferred_element_type=F32)
        hidden = (gate / (1.0 + jnp.exp(-gate)) * up).astype(BF16)

        def share_of(t):
            columns = pl.ds(pl.multiple_of(t * WIDTH, WIDTH), WIDTH)
            return jnp.dot(hidden, wd[:, columns], preferred_element_type=F32)

        for s in order:
            ds[at.at_y(s), parts[n]] = share_of(at.at_y(s)).astype(BF16)
            share(n, s).start()
        own.append(share_of(y))
    for n in range(PARTS):
        for s in order:
            pooled(n, s).wait_send()
    for n in range(PARTS):
        total = own[n]
        for s in order:
            share_came(n, s).wait_recv()
            total = total + rs[at.at_y(-s), parts[n]].astype(F32)
        out_ref[parts[n]] = (mixed_ref[y, parts[n]] + total).astype(BF16)
    for n in range(PARTS):
        for s in order:
            share(n, s).wait_send()


def local(
    compound_tokens,
    pocket_tokens,
    token_count,
    pair_compound,
    pair_conformer,
    owner,
    w_query,
    w_key,
    w_value,
    w_out,
    norm_gain,
    w_gate,
    w_up,
    w_down,
):
    smem = pl.BlockSpec(memory_space=pltpu.SMEM)
    vmem = pl.BlockSpec(memory_space=pltpu.VMEM)
    hbm = pl.BlockSpec(memory_space=pltpu.HBM)
    dma = pltpu.SemaphoreType.DMA
    gather_sems = [
        dma((2, NX)), dma((2, NX, NZ)), dma((2, NZ)), dma((2, NZ, NX)),
        dma((2, NZ)), dma((2, NZ)),
    ]
    return pl.pallas_call(
        kernel,
        out_shape=jax.ShapeDtypeStruct((PAIRS, WIDTH), BF16),
        in_specs=[smem] * 4 + [vmem] * 2 + [hbm] * 9,
        out_specs=vmem,
        scratch_shapes=[
            pltpu.VMEM((2, NZ, NX, KEYS, WIDTH), BF16),
            pltpu.VMEM((2, NZ, NX, KEYS, WIDTH), BF16),
            pltpu.VMEM((NT, CMP * TOK, WIDTH), BF16),
            pltpu.VMEM((NT, WIDTH, D), BF16),
            pltpu.VMEM((KEYS, D), BF16),
            pltpu.VMEM((D, WIDTH), BF16),
            pltpu.VMEM((D, WIDTH), BF16),
            pltpu.VMEM((D, WIDTH), BF16),
            pltpu.VMEM((D, FFN), BF16),
            pltpu.VMEM((D, FFN), BF16),
            pltpu.VMEM((FFN, D), BF16),
            pltpu.VMEM((CMP, WIDTH, WIDTH), BF16),
            pltpu.VMEM((CMP, 1, WIDTH), F32),
            pltpu.VMEM((16, D), F32),
            pltpu.VMEM((BATCH, KEYS, WIDTH), F32),
            pltpu.VMEM((BATCH, KEYS, WIDTH), BF16),
            pltpu.VMEM((PAIRS, 16, KEYS), BF16),
            pltpu.VMEM((NT, PAIRS, WIDTH), BF16),
            pltpu.VMEM((NT, PAIRS, WIDTH), F32),
            pltpu.VMEM((NT, PAIRS, WIDTH), BF16),
            pltpu.VMEM((NT, PAIRS, WIDTH), BF16),
            dma((9,)),
        ]
        + gather_sems
        + gather_sems
        + [dma((2, 2, 2, 4)), dma((2, 2, 2, 4)), dma((2, NT)), dma((2, PARTS, 7)), dma((2, PARTS, 7))],
        compiler_params=pltpu.CompilerParams(
            collective_id=0, has_side_effects=True, vmem_limit_bytes=62 << 20
        ),
        name="conformer_attention",
    )(
        token_count, pair_compound, pair_conformer.reshape(-1), owner, pair_compound,
        norm_gain.reshape(1, -1), compound_tokens, pocket_tokens, w_query, w_key, w_value,
        w_out, w_gate, w_up, w_down,
    )


def solution(mesh):
    return jax.shard_map(
        local,
        mesh=mesh,
        in_specs=(
            P("pocket", "tensor"),
            P("pocket", None),
            P("pocket"),
            P("pocket", None),
            P("pocket", None),
            P(),
            P(None, "tensor"),
            P(None, "tensor"),
            P(None, "tensor"),
            P("tensor", None),
            P(),
            P(None, "tensor"),
            P(None, "tensor"),
            P("tensor", None),
        ),
        out_specs=P("pocket", "tensor"),
        check_vma=False,
    )
```
